32 devices in a mesh: band: 2 (over x), tile: 16 (over z, y, core).
Axes of the slice: x: 2, y: 2, z: 4, core: 2. Of those that a mesh axis runs over, the one named last changes fastest.
Arguments:
- vis: bfloat16 [2, 512, 64, 128], P('band', 'tile'), may hold values from -6 to 6
- coords: bfloat16 [512, 2, 128], P('tile'), may hold values from -8 to 8
- block_fill: int32 [512], P('tile'), may hold values from 1 to 128, as said below
- block_sub: int32 [512], P('tile'), may hold values from 0 to 127, as said below
- sub_pos: int32 [128, 2], replicated, may hold values from 0 to 8160, as said below
- sub_plane: int32 [128], replicated, may hold values from 0 to 1
- freq: float32 [2, 32], P('band'), may hold values from 0.85 to 1.15
- plane_w: float32 [2, 2], P('band'), may hold values from -4 to 4
Outputs:
- image: float32 [2, 8192, 128], P('band', 'tile')
The draws below stay inside these ranges and needn't reach their ends.
Inputs may be any that keep to these rules, and one draw needn't show every extreme that they name: `sub_pos`: subgrid s has its first row in panel s mod 16 (panels of 512 rows); first rows are at most 8160, first columns at most 32. `block_sub`: of the 32 blocks of one device, at most 2 feed subgrids whose first row lies in one panel; in every draw one panel receives 2 blocks from every device. Rows at or after block_fill of a block are padding; every device has a full block.
All inputs are finite; a program needn't handle non-finite values.
Results may differ from the reference program's by a relative error of at most 0.0054.
Values may be sent and summed in bfloat16 or wider, within the bound.
No kernel may reach another device: no remote copies, remote signals or barrier semaphores. Data moves between devices by JAX's collectives and lax.ppermute only.
A program may use at most 128 MiB of HBM per device.

```python
import math
import jax
import jax.numpy as jnp
from jax import lax

CH = 32
SUB = 32
BROWS = 128
NBLK = 32
CAP = 2
SPP = 8
NV = 8192
NCOL = 64
PLANES = 2
BANDS = 2
OWNERS = 16
BLOCKS = 512
NSUB = 128


def draw_block_sub(key, part):
    hot_key = jax.random.fold_in(key, 11)
    turn_key = jax.random.fold_in(key, 12)
    rotate_key = jax.random.fold_in(key, 13)
    which_key = jax.random.fold_in(key, 14)
    hot = jax.random.randint(hot_key, (), 0, OWNERS)
    base_turn = jax.random.randint(turn_key, (), 0, OWNERS - 1)
    offset = (jnp.arange(OWNERS) + base_turn) % (OWNERS - 1)
    rotate = jax.random.randint(rotate_key, (OWNERS,), 0, NBLK)
    index = jnp.arange(NBLK)
    order = (index[None, :] + rotate[:, None]) % NBLK
    other = (hot + 1 + (offset[:, None] + order - CAP) % (OWNERS - 1)) % OWNERS
    owner = jnp.where(order < CAP, hot, other)
    which = jax.random.randint(which_key, (OWNERS, NBLK), 0, SPP)
    which = jnp.where((order == 0) | (order == CAP), 0, which)
    return (owner + OWNERS * which).reshape(BLOCKS).astype(jnp.int32)


def draw_sub_pos(key, part):
    row_key = jax.random.fold_in(key, 21)
    col_key = jax.random.fold_in(key, 22)
    index = jnp.arange(NSUB)
    panel_rows = NV // OWNERS
    offset = jax.random.randint(row_key, (NSUB,), 0, panel_rows)
    offset = jnp.where(index < OWNERS, panel_rows - SUB // 2, offset)
    first_row = jnp.minimum(index % OWNERS * panel_rows + offset, NV - SUB)
    first_row = jnp.where(index == NSUB - 1, NV - SUB, first_row)
    first_col = jax.random.randint(col_key, (NSUB,), 0, NCOL - SUB + 1)
    return jnp.stack([first_row, first_col], axis=1).astype(jnp.int32)


def draw_block_fill(key, part):
    fill_key = jax.random.fold_in(key, 31)
    drawn = jax.random.randint(fill_key, (BLOCKS,), 1, BROWS + 1)
    index = jnp.arange(BLOCKS)
    full = index % NBLK == index // NBLK % NBLK
    return jnp.where(full, BROWS, drawn).astype(jnp.int32)


def with_ends(entries, rng, low, largest):
    longest = entries.shape.index(max(entries.shape))
    spots = []
    for shift in (0, 1):
        where = [jax.random.randint(jax.random.fold_in(rng, axis), (), 0, length) for axis, length in enumerate(entries.shape)]
        where[longest] = (where[longest] + shift) % entries.shape[longest]
        spots.append(tuple(where))
    return entries.at[spots[0]].set(low).at[spots[1]].set(largest)


def level_of(rng, shape, cuts, least, high):
    gain = 1.0
    for position, parts in cuts:
        heights = jax.random.uniform(jax.random.fold_in(jax.random.fold_in(rng, 6), position), (parts,), jnp.float32, least / len(cuts), high / len(cuts))
        gain = gain * jnp.repeat(jnp.exp(heights), shape[position] // parts).reshape((-1,) + (1,) * (len(shape) - 1 - position))
    return gain


def normal_values(key, shape, scale, limit, cuts=(), held_as=jnp.bfloat16):
    result = jax.random.normal(key, shape, jnp.float32) * scale
    if len(cuts) > 0:
        result = level_of(key, shape, cuts, -0.22, 0.18) * result
    return jnp.clip(result, min=-limit, max=limit).astype(held_as)


def setup_inputs(seed: int = 0) -> dict:
    key_of = jax.random.split(jax.random.key(seed), 9)
    vis = normal_values(key_of[0], (BANDS, BLOCKS, 2 * CH, BROWS), 1.0, 6.0, ((0, 2), (1, 16)))
    coords = jnp.clip(jax.random.uniform(key_of[1], (BLOCKS, 2, BROWS), jnp.float32, -8.0, 8.0) * level_of(key_of[1], (BLOCKS, 2, BROWS), ((0, 16),), -0.4, 0.0), -8.0, 8.0).astype(jnp.bfloat16)
    block_fill = draw_block_fill(jax.random.fold_in(key_of[8], 71), 0)
    block_sub = draw_block_sub(jax.random.fold_in(key_of[8], 71), 0)
    sub_pos = draw_sub_pos(jax.random.fold_in(key_of[8], 71), 0)
    sub_plane = with_ends(jax.random.randint(key_of[5], (NSUB,), 0, PLANES), jax.random.fold_in(key_of[5], 1), 0, PLANES - 1).astype(jnp.int32)
    freq = jnp.clip(0.85 + 0.29999995 * jax.random.uniform(key_of[6], (BANDS, CH), jnp.float32) ** level_of(key_of[6], (BANDS, CH), ((0, 2),), -0.2, 0.2), 0.85, 1.15)
    plane_w = jnp.clip(jax.random.uniform(key_of[7], (BANDS, PLANES), jnp.float32, -4.0, 4.0) * level_of(key_of[7], (BANDS, PLANES), ((0, 2),), -0.4, 0.0), -4.0, 4.0)
    return {"vis": vis, "coords": coords, "block_fill": block_fill, "block_sub": block_sub, "sub_pos": sub_pos, "sub_plane": sub_plane, "freq": freq, "plane_w": plane_w}


def form_patches(vis_blocks, coord_blocks, fill_blocks, freq_band):
    count = vis_blocks.shape[0]
    group = 8 if count % 8 == 0 else 4
    chans = freq_band.shape[0]
    rows = vis_blocks.shape[2]
    side = SUB
    pixel = (jnp.arange(side).astype(jnp.float32) - side // 2) / side
    taper = 1.0 - 0.9 * ((2 * jnp.arange(side) + 1 - side).astype(jnp.float32) / side) ** 2
    weight = taper[:, None] * taper[None, :]
    turns = jnp.arange(side)[:, None] * jnp.arange(side)[None, :] % side
    dft_angle = -2.0 * math.pi / side * turns.astype(jnp.float32)
    dft_re = jnp.cos(dft_angle)
    dft_im = jnp.sin(dft_angle)
    scale = 1.0 / math.sqrt(chans * rows)
    highest = lax.Precision.HIGHEST

    def one_group(items):
        vis_g, coord_g, fill_g = items
        live = (jnp.arange(rows)[None, :] < fill_g[:, None]).astype(jnp.float32)
        coord_f = coord_g.astype(jnp.float32)
        shift_u = (freq_band[None, :, None] * coord_f[:, 0:1, :]).reshape(group, 1, chans * rows)
        shift_v = (freq_band[None, :, None] * coord_f[:, 1:2, :]).reshape(group, 1, chans * rows)
        angle_u = 2.0 * math.pi * pixel[None, :, None] * shift_u
        angle_v = 2.0 * math.pi * pixel[None, :, None] * shift_v
        amp = live[:, None, :] * scale
        vis_re = (vis_g[:, :chans, :].astype(jnp.float32) * amp).reshape(group, 1, chans * rows)
        vis_im = (vis_g[:, chans:, :].astype(jnp.float32) * amp).reshape(group, 1, chans * rows)
        cos_u = jnp.cos(angle_u)
        sin_u = jnp.sin(angle_u)
        left = jnp.concatenate([vis_re * cos_u - vis_im * sin_u, vis_re * sin_u + vis_im * cos_u], axis=1).astype(jnp.bfloat16)
        right = jnp.concatenate([jnp.cos(angle_v), jnp.sin(angle_v)], axis=1).astype(jnp.bfloat16)
        left_f = lax.optimization_barrier(left).astype(jnp.float32)
        right_f = lax.optimization_barrier(right).astype(jnp.float32)
        prod = jnp.einsum('gik,gjk->gij', left_f, right_f)
        sky_re = (prod[:, :side, :side] - prod[:, side:, side:]) * weight
        sky_im = (prod[:, :side, side:] + prod[:, side:, :side]) * weight
        half_re = jnp.einsum('pi,gij->gpj', dft_re, sky_re, precision=highest) - jnp.einsum('pi,gij->gpj', dft_im, sky_im, precision=highest)
        half_im = jnp.einsum('pi,gij->gpj', dft_re, sky_im, precision=highest) + jnp.einsum('pi,gij->gpj', dft_im, sky_re, precision=highest)
        out_re = jnp.einsum('gpj,qj->gpq', half_re, dft_re, precision=highest) - jnp.einsum('gpj,qj->gpq', half_im, dft_im, precision=highest)
        out_im = jnp.einsum('gpj,qj->gpq', half_re, dft_im, precision=highest) + jnp.einsum('gpj,qj->gpq', half_im, dft_re, precision=highest)
        return (jnp.stack([out_re, out_im], axis=2) / side).astype(jnp.bfloat16)
    shaped = (vis_blocks.reshape(count // group, group, 2 * chans, rows), coord_blocks.reshape(count // group, group, 2, rows), fill_blocks.reshape(count // group, group))
    made = lax.map(one_group, shaped)
    return made.reshape(count, side, 2, side)

def place(canvas, patches, subs, sub_pos, sub_plane, row_base):
    count = patches.shape[0]
    side = patches.shape[1]
    ids = jnp.arange(sub_pos.shape[0])
    match = subs[:, None] == ids[None, :]
    top = lax.optimization_barrier(jnp.sum(jnp.where(match, sub_pos[None, :, 0], 0), axis=1)) - row_base
    first_col = lax.optimization_barrier(jnp.sum(jnp.where(match, sub_pos[None, :, 1], 0), axis=1))
    plane = lax.optimization_barrier(jnp.sum(jnp.where(match, sub_plane[None, :], 0), axis=1))
    onehot = (plane[:, None] == jnp.arange(PLANES)[None, :]).astype(jnp.float32)
    values = lax.optimization_barrier(patches).astype(jnp.float32)
    spread = (values[..., None] * onehot[:, None, None, None, :]).reshape(count, side, 2, side * PLANES)
    row_idx = top[:, None] + jnp.arange(side)[None, :]
    col_idx = first_col[:, None] * PLANES + jnp.arange(side * PLANES)[None, :]
    return canvas.at[row_idx[:, :, None, None], jnp.arange(2)[None, None, :, None], col_idx[:, None, None, :]].add(spread, mode='drop')

def finish(spec_re, spec_im, first_row, w_band):
    count = spec_re.shape[0]
    qpos = (first_row + jnp.arange(count)).astype(jnp.float32) / NV - 0.5
    cpos = jnp.arange(NCOL).astype(jnp.float32) / NCOL - 0.5
    phase = 2.0 * math.pi * w_band[None, None, :] * ((qpos * qpos)[:, None, None] + (cpos * cpos)[None, :, None])
    part_re = spec_re.reshape(count, NCOL, PLANES)
    part_im = spec_im.reshape(count, NCOL, PLANES)
    cosine = jnp.cos(phase)
    sine = jnp.sin(phase)
    out_re = lax.optimization_barrier(jnp.sum(part_re * cosine - part_im * sine, axis=2))
    out_im = lax.optimization_barrier(jnp.sum(part_re * sine + part_im * cosine, axis=2))
    return jnp.concatenate([out_re, out_im], axis=1) / math.sqrt(NV)

def reference(vis, coords, block_fill, block_sub, sub_pos, sub_plane, freq, plane_w):

    def one_band(items):
        vis_band, freq_band, w_band = items
        patches = form_patches(vis_band, coords, block_fill, freq_band)
        canvas = place(jnp.zeros((NV, 2, NCOL * PLANES), jnp.float32), patches, block_sub, sub_pos, sub_plane, 0)
        grid = lax.optimization_barrier(canvas.astype(jnp.bfloat16)).astype(jnp.float32)
        spectrum = jnp.fft.fft(grid[:, 0, :] + 1j * grid[:, 1, :], axis=0)
        return finish(jnp.real(spectrum).astype(jnp.float32), jnp.imag(spectrum).astype(jnp.float32), 0, w_band)
    return lax.map(one_band, (vis, freq, plane_w))
```

```python
import functools
import math

import jax
import jax.numpy as jnp
import numpy as np
from jax import lax
from jax.experimental import pallas as pl
from jax.experimental.pallas import tpu as pltpu
from jax.sharding import PartitionSpec as P

SUB = 32
HALF = SUB // 2
CAP = 2
NV = 8192
NCOL = 64
SPP = 8
ROWS = 48
F32 = jnp.float32
BF16 = jnp.bfloat16


def poly(x2, coefs):
    acc = jnp.full_like(x2, coefs[-1])
    for coef in coefs[-2::-1]:
        acc = acc * x2 + coef
    return acc


def sincos(x, terms):
    x2 = x * x
    sine = x * poly(x2, [(-1.0) ** k / math.factorial(2 * k + 1) for k in range(terms)])
    cosine = poly(x2, [(-1.0) ** k / math.factorial(2 * k) for k in range(terms + 1)])
    return sine, cosine


def cis(turns):
    sine, cosine = sincos(turns * math.pi, 6)
    return 1.0 - 2.0 * sine * sine, 2.0 * sine * cosine


def column_matrix():
    p = np.arange(SUB)[:, None]
    h = np.arange(HALF)[None, :]
    taper = 1.0 - 0.9 * ((2 * h + 1) / SUB) ** 2
    angle = 2.0 * np.pi * p * (h + 0.5) / SUB
    return np.concatenate([2 * taper * np.cos(angle), 2 * taper * np.sin(angle)], axis=1)


def fold_matrix():
    mt = column_matrix().T
    out = np.zeros((2, 2, 2, SUB, 2, 2, SUB))
    for j in range(2):
        for slot in range(2):
            for part in range(2):
                out[j, slot, part, :, part, j, :] = mt
    return out.reshape(8 * SUB, 4 * SUB).astype(np.float32)


def sky_kernel(tiles, sub_ref, fill_ref, freq_ref, vis_ref, coord_ref, out_ref,
               blk, count, trig, volt, left, right):
    panel = pl.program_id(0)
    blocks = vis_ref.shape[0]
    chans = vis_ref.shape[1] // 2
    lanes = vis_ref.shape[2]

    @pl.when(panel == 0)
    def _():
        @pl.loop(0, tiles)
        def _(i):
            count[i] = 0
            for j in range(CAP):
                blk[CAP * i + j] = -1

        @pl.loop(0, blocks)
        def _(b):
            p = lax.rem(sub_ref[b], tiles)
            have = count[p]
            blk[CAP * p + have] = b
            count[p] = have + 1

    row = lax.broadcasted_iota(jnp.int32, (chans, chans), 0)
    col = lax.broadcasted_iota(jnp.int32, (chans, chans), 1)
    freq = jnp.sum(jnp.where(row == col, freq_ref[...], 0.0), axis=1, keepdims=True)
    lane = lax.broadcasted_iota(jnp.int32, (chans, lanes), 1)
    lane16 = lax.broadcasted_iota(jnp.int32, (ROWS - SUB, 4 * SUB), 1)
    pieces = []
    ids = jnp.zeros((ROWS - SUB, 4 * SUB), F32)
    for slot in range(CAP):
        which = blk[CAP * panel + slot]
        b = jnp.maximum(which, 0)
        live = jnp.where(which < 0, 0, fill_ref[b])
        ids = jnp.where(lane16 // (2 * SUB) == slot, (sub_ref[b] // tiles).astype(F32), ids)
        coord = coord_ref[b].astype(F32)
        heads = []
        for axis in range(2):
            angle = freq * coord[axis : axis + 1, :] * (math.pi / SUB)
            sine, cosine = sincos(angle, 5)
            heads.append((cosine, sine))
            twice = 2.0 - 4.0 * sine * sine
            now = (cosine, sine)
            last = (cosine, -sine)
            for h in range(HALF):
                for part in range(2):
                    start = ((axis * 2 + part) * HALF + h) * chans
                    trig[slot, start : start + chans, :] = now[part]
                now, last = tuple(twice * a - z for a, z in zip(now, last)), now
        (cu, su), (cv, sv) = heads
        turn_re = cu * cv - su * sv
        turn_im = su * cv + cu * sv
        volts = vis_ref[b].astype(F32)
        keep = lane < live
        v_re = jnp.where(keep, volts[:chans], 0.0)
        v_im = jnp.where(keep, volts[chans:], 0.0)
        volt[slot, :chans, :] = v_re * turn_re + v_im * turn_im
        volt[slot, chans:, :] = v_im * turn_re - v_re * turn_im
        for c in range(chans):
            t = [trig[slot, pl.ds(k * HALF * chans + c, HALF, stride=chans), :] for k in range(4)]
            w_re = volt[slot, c : c + 1, :]
            w_im = volt[slot, chans + c : chans + c + 1, :]
            at = slice(c * lanes, (c + 1) * lanes)
            left[slot, :, at] = jnp.concatenate(
                [w_re * t[0], w_re * t[1], w_im * t[0], w_im * t[1]], axis=0
            ).astype(BF16)
            right[slot, :, at] = jnp.concatenate([t[2], t[3]], axis=0).astype(BF16)
        sky = lax.dot_general(
            left[slot], right[slot], (((1,), (1,)), ((), ())), preferred_element_type=F32
        )
        pieces += [sky[:SUB], sky[SUB:]]
    out_ref[0, :SUB, :] = jnp.concatenate(pieces, axis=1).astype(BF16)
    out_ref[0, SUB:, :] = ids.astype(BF16)


def form_skies(vis, coords, block_fill, block_sub, freq, tiles):
    blocks, parts, lanes = vis.shape
    chans = parts // 2
    whole = lambda shape: pl.BlockSpec(shape, lambda i, *_: (0,) * len(shape))
    return pl.pallas_call(
        functools.partial(sky_kernel, tiles),
        grid_spec=pltpu.PrefetchScalarGridSpec(
            num_scalar_prefetch=2,
            grid=(tiles,),
            in_specs=[whole(freq.shape), whole(vis.shape), whole(coords.shape)],
            out_specs=pl.BlockSpec((1, ROWS, 4 * SUB), lambda i, *_: (i, 0, 0)),
            scratch_shapes=[
                pltpu.SMEM((CAP * tiles,), jnp.int32),
                pltpu.SMEM((tiles,), jnp.int32),
                pltpu.VMEM((CAP, 4 * HALF * chans, lanes), F32),
                pltpu.VMEM((CAP, parts, lanes), F32),
                pltpu.VMEM((CAP, 2 * SUB, chans * lanes), BF16),
                pltpu.VMEM((CAP, SUB, chans * lanes), BF16),
            ],
        ),
        out_shape=jax.ShapeDtypeStruct((tiles, ROWS, 4 * SUB), BF16),
        compiler_params=pltpu.CompilerParams(vmem_limit_bytes=32 * 2**20),
        name="skies",
    )(block_sub, block_fill, freq, vis, coords)


def sum_kernel(norm, me_ref, pos_ref, plane_ref, w_ref, got_ref, fold_ref, out_ref, acc):
    tiles = got_ref.shape[0]
    me = me_ref[0]
    acc[...] = jnp.zeros_like(acc)
    for sender in range(tiles):
        data = got_ref[sender, :SUB, :].astype(F32)
        ids = got_ref[sender, SUB:, :].astype(F32)[:1]
        for sub in range(SPP):
            at = slice(sub // 2 * SUB, (sub // 2 + 1) * SUB)
            lanes = slice(sub % 2 * 4 * SUB, (sub % 2 + 1) * 4 * SUB)
            acc[at, lanes] += jnp.where(ids == sub, data, 0.0)
    made = lax.dot_general(
        acc[...], fold_ref[...], (((1,), (0,)), ((), ())),
        precision=lax.Precision.HIGHEST, preferred_element_type=F32,
    )
    turned = pltpu.roll(made, 2 * SUB, 1)
    lane = lax.broadcasted_iota(jnp.int32, (8, 4 * SUB), 1)
    column = lane % SUB
    odd = lane // SUB % 2 == 1
    for pair in range(SPP // 2):
        a = (2 * pair) * tiles + me
        b = (2 * pair + 1) * tiles + me
        first = jnp.where(odd, pos_ref[b, 1], pos_ref[a, 1])
        w = jnp.where(odd, w_ref[0, plane_ref[b]], w_ref[0, plane_ref[a]])
        x = (first + column).astype(F32) / NCOL - 0.5
        steps = lax.rem(31 * column, 64).astype(F32) / 64
        turns = w * (x * x) - steps
        c_re, c_im = cis(turns - jnp.round(turns))
        c_re = (c_re * norm)[:1]
        c_im = (jnp.where(lane < 2 * SUB, -c_im, c_im) * norm)[:1]
        at = slice(pair * SUB, (pair + 1) * SUB)
        out_ref[at, :] = (made[at] * c_re + turned[at] * c_im).astype(BF16)


def sum_subgrids(got, me, sub_pos, sub_plane, w_band, norm):
    smem = pl.BlockSpec(memory_space=pltpu.SMEM)
    vmem = pl.BlockSpec(memory_space=pltpu.VMEM)
    return pl.pallas_call(
        functools.partial(sum_kernel, norm),
        in_specs=[smem, smem, smem, smem, vmem, vmem],
        out_specs=vmem,
        out_shape=jax.ShapeDtypeStruct((SPP // 2 * SUB, 4 * SUB), BF16),
        scratch_shapes=[pltpu.VMEM((SPP // 2 * SUB, 8 * SUB), F32)],
        compiler_params=pltpu.CompilerParams(vmem_limit_bytes=32 * 2**20),
        name="sums",
    )(me, sub_pos, sub_plane, w_band, got, jnp.asarray(fold_matrix()))


def table_kernel(tiles, me_ref, gy_ref, w_ref, mat_ref, out_ref, turn_re, turn_im, base_re, base_im):
    panel = pl.program_id(0)
    rows = out_ref.shape[1] // 2
    subs = gy_ref.shape[1]

    @pl.when(panel == 0)
    def _():
        first = me_ref[0] * rows
        q = first + lax.broadcasted_iota(jnp.int32, (rows, subs), 0)
        steps = (q * gy_ref[...] + NV // 2) & (NV - 1)
        pos = q.astype(F32) / NV - 0.5
        turns = (NV // 2 - steps).astype(F32) / NV + w_ref[...] * (pos * pos)
        for ref, value in zip((turn_re, turn_im), cis(turns - jnp.round(turns))):
            high = value.astype(BF16)
            ref[:, :subs] = high
            ref[:, subs:] = (value - high.astype(F32)).astype(BF16)
        q = first + lax.broadcasted_iota(jnp.int32, (rows, SUB), 0)
        r = lax.broadcasted_iota(jnp.int32, (rows, SUB), 1)
        steps = ((q + 31 * NV // 64) * r + NV // 2) & (NV - 1)
        for ref, value in zip((base_re, base_im), cis((NV // 2 - steps).astype(F32) / NV)):
            ref[...] = lax.dot_general(
                value, mat_ref[...], (((1,), (0,)), ((), ())),
                precision=lax.Precision.HIGHEST, preferred_element_type=F32,
            )

    row = lax.broadcasted_iota(jnp.int32, (2 * subs, SPP * SUB), 0)
    col = lax.broadcasted_iota(jnp.int32, (2 * subs, SPP * SUB), 1)
    pick = jnp.where(row % subs == panel * SPP + col // SUB, 1.0, 0.0).astype(BF16)
    wide_re = jnp.dot(turn_re[...], pick, preferred_element_type=F32)
    wide_im = jnp.dot(turn_im[...], pick, preferred_element_type=F32)
    for k in range(2):
        at = slice(k * 4 * SUB, (k + 1) * 4 * SUB)
        out_ref[0, :rows, at] = (wide_re[:, at] * base_re[...] - wide_im[:, at] * base_im[...]).astype(BF16)
        out_ref[0, rows:, at] = (wide_re[:, at] * base_im[...] + wide_im[:, at] * base_re[...]).astype(BF16)


def make_table(me, sub_pos, sub_plane, w_band, tiles):
    rows = NV // tiles
    subs = sub_pos.shape[0]
    gy = sub_pos[:, 0].reshape(SPP, tiles).T.reshape(1, subs)
    w = jnp.where(sub_plane == 0, w_band[0, 0], w_band[0, 1]).reshape(SPP, tiles).T.reshape(1, subs)
    mat = np.tile(column_matrix(), (1, 4)).astype(np.float32)
    whole = lambda shape: pl.BlockSpec(shape, lambda i: (0,) * len(shape))
    return pl.pallas_call(
        functools.partial(table_kernel, tiles),
        grid=(tiles,),
        in_specs=[pl.BlockSpec(memory_space=pltpu.SMEM), whole(gy.shape), whole(w.shape), whole(mat.shape)],
        out_specs=pl.BlockSpec((1, 2 * rows, SPP * SUB), lambda i: (i, 0, 0)),
        out_shape=jax.ShapeDtypeStruct((tiles, 2 * rows, SPP * SUB), BF16),
        scratch_shapes=[
            pltpu.VMEM((rows, 2 * subs), BF16),
            pltpu.VMEM((rows, 2 * subs), BF16),
            pltpu.VMEM((rows, 4 * SUB), F32),
            pltpu.VMEM((rows, 4 * SUB), F32),
        ],
        compiler_params=pltpu.CompilerParams(vmem_limit_bytes=32 * 2**20),
        name="table",
    )(me, gy, w, jnp.asarray(mat))


def image_kernel(tiles, pos_ref, table_ref, z_ref, out_ref, acc, canvas):
    panel = pl.program_id(0)
    rows = out_ref.shape[0]
    lane = lax.broadcasted_iota(jnp.int32, (SUB, 4 * SUB), 1)
    for sub in range(SPP):
        first = pos_ref[sub * tiles + panel, 1]
        pair = z_ref[0, sub // 2 * SUB : (sub // 2 + 1) * SUB, :].astype(F32)
        moved = pltpu.roll(pair, (first - sub % 2 * SUB + 4 * SUB) % (4 * SUB), 1)
        place = (lane & (NCOL - 1)) - first
        canvas[sub * SUB : (sub + 1) * SUB, :] = jnp.where(
            (place >= 0) & (place < SUB), moved, 0.0
        ).astype(BF16)
    part = jnp.dot(table_ref[0], canvas[...], preferred_element_type=F32)

    @pl.when(panel == 0)
    def _():
        acc[...] = part

    @pl.when(panel > 0)
    def _():
        acc[...] += part

    @pl.when(panel == tiles - 1)
    def _():
        lanes = lax.broadcasted_iota(jnp.int32, (rows, 4 * SUB), 1)
        turned = pltpu.roll(acc[rows:, :], 2 * SUB, 1)
        out_ref[...] = acc[:rows, :] + jnp.where(lanes < 2 * SUB, -turned, turned)


def make_image(table, z, sub_pos):
    tiles, rows2, depth = table.shape
    rows = rows2 // 2
    return pl.pallas_call(
        functools.partial(image_kernel, tiles),
        grid_spec=pltpu.PrefetchScalarGridSpec(
            num_scalar_prefetch=1,
            grid=(tiles,),
            in_specs=[
                pl.BlockSpec((1, rows2, depth), lambda i, *_: (i, 0, 0)),
                pl.BlockSpec((1,) + z.shape[1:], lambda i, *_: (i, 0, 0)),
            ],
            out_specs=pl.BlockSpec((rows, 4 * SUB), lambda i, *_: (0, 0)),
            scratch_shapes=[pltpu.VMEM((rows2, 4 * SUB), F32), pltpu.VMEM((depth, 4 * SUB), BF16)],
        ),
        out_shape=jax.ShapeDtypeStruct((rows, 4 * SUB), F32),
        compiler_params=pltpu.CompilerParams(vmem_limit_bytes=32 * 2**20),
        name="image",
    )(sub_pos, table, z)


def shards(vis, coords, block_fill, block_sub, sub_pos, sub_plane, freq, plane_w):
    tiles = lax.axis_size("tile")
    me = lax.axis_index("tile").reshape(1)
    norm = 1.0 / (math.sqrt(vis.shape[2] // 2 * vis.shape[3]) * SUB * math.sqrt(NV))
    skies = form_skies(vis[0], coords, block_fill, block_sub, freq, tiles)
    table = make_table(me, sub_pos, sub_plane, plane_w, tiles)
    got = lax.all_to_all(skies, "tile", split_axis=0, concat_axis=0, tiled=True)
    z = sum_subgrids(got, me, sub_pos, sub_plane, plane_w, norm)
    z = lax.all_to_all(
        jnp.broadcast_to(z[None], (tiles,) + z.shape), "tile", split_axis=0, concat_axis=0, tiled=True
    )
    return make_image(table, z, sub_pos)[None]


def solution(mesh):
    return jax.shard_map(
        shards,
        mesh=mesh,
        in_specs=(
            P("band", "tile", None, None),
            P("tile", None, None),
            P("tile"),
            P("tile"),
            P(),
            P(),
            P("band", None),
            P("band", None),
        ),
        out_specs=P("band", "tile", None),
        check_vma=False,
    )
```

```python
import functools
import math

import jax
import jax.numpy as jnp
import numpy as np
from jax import lax
from jax.experimental import pallas as pl
from jax.experimental.pallas import tpu as pltpu
from jax.sharding import PartitionSpec as P

SUB = 32
HALF = SUB // 2
CAP = 2
NV = 8192
NCOL = 64
SPP = 8
ROWS = 48
GROUP = 8
LIMIT = 60 * 2**20
F32 = jnp.float32
BF16 = jnp.bfloat16


def poly(x2, coefs):
    acc = jnp.full_like(x2, coefs[-1])
    for coef in coefs[-2::-1]:
        acc = acc * x2 + coef
    return acc


def sincos(x, terms):
    x2 = x * x
    sine = x * poly(x2, [(-1.0) ** k / math.factorial(2 * k + 1) for k in range(terms)])
    cosine = poly(x2, [(-1.0) ** k / math.factorial(2 * k) for k in range(terms + 1)])
    return sine, cosine


def cis(turns):
    sine, cosine = sincos(turns * math.pi, 6)
    return 1.0 - 2.0 * sine * sine, 2.0 * sine * cosine


def column_matrix():
    p = np.arange(SUB)[:, None]
    h = np.arange(HALF)[None, :]
    taper = 1.0 - 0.9 * ((2 * h + 1) / SUB) ** 2
    angle = 2.0 * np.pi * p * (h + 0.5) / SUB
    return np.concatenate([2 * taper * np.cos(angle), 2 * taper * np.sin(angle)], axis=1)


def fold_matrix():
    mt = column_matrix().T
    out = np.zeros((2, 2, 2, SUB, 2, 2, SUB))
    for j in range(2):
        for slot in range(2):
            for part in range(2):
                out[j, slot, part, :, part, j, :] = mt
    return out.reshape(8 * SUB, 4 * SUB).astype(np.float32)


def pick_matrices():
    iota = lambda shape, dim: lax.broadcasted_iota(jnp.int32, shape, dim)
    one = lambda mask: jnp.where(mask, 1.0, 0.0).astype(BF16)
    shape = (SUB * GROUP, 4 * SUB)
    k, lane = iota(shape, 0), iota(shape, 1)
    fits = (k // GROUP == lane % SUB) & (k % CAP == lane // (2 * SUB))
    place = [one(fits & (lane // SUB % 2 == part)) for part in range(2)]
    shape = (GROUP // CAP * SUB, SUB * GROUP)
    r, k = iota(shape, 0), iota(shape, 1)
    return place, one((r % SUB == k // GROUP) & (r // SUB == k % GROUP // CAP))


def sky_kernel(tiles, sub_hbm, fill_hbm, freq_hbm, vis_hbm, coord_hbm, out_ref,
               sub_ref, fill_ref, freq_ref, vis_ref, coord_ref, blk, count, sems, volt, uv, acc, *bufs):
    blocks = vis_ref.shape[0]
    chans = vis_ref.shape[1] // 2
    lanes = vis_ref.shape[2]
    step = 2 * chans + 1
    pairs = ((sub_hbm, sub_ref), (fill_hbm, fill_ref), (freq_hbm, freq_ref), (coord_hbm, coord_ref), (vis_hbm, vis_ref))
    copies = [pltpu.make_async_copy(a, b, sems.at[i]) for i, (a, b) in enumerate(pairs)]
    for copy in copies:
        copy.start()

    @pl.loop(0, tiles)
    def _(i):
        count[i] = 0
        for j in range(CAP):
            blk[CAP * i + j] = -1

    for copy in copies:
        copy.wait()

    @pl.loop(0, blocks)
    def _(b):
        p = sub_ref[b] & (tiles - 1)
        have = count[p]
        blk[CAP * p + have] = b
        count[p] = have + 1

    place, gather = pick_matrices()
    lane = lax.broadcasted_iota(jnp.int32, (GROUP, lanes), 1)
    row = lax.broadcasted_iota(jnp.int32, (GROUP, lanes), 0)
    lane16 = lax.broadcasted_iota(jnp.int32, (ROWS - SUB, 4 * SUB), 1)
    same = (lax.broadcasted_iota(jnp.int32, (2 * SUB * GROUP, SUB * GROUP), 0) % GROUP
            == lax.broadcasted_iota(jnp.int32, (2 * SUB * GROUP, SUB * GROUP), 1) % GROUP)

    @pl.loop(0, CAP * tiles // GROUP)
    def _(group):
        live = jnp.zeros((GROUP, lanes), jnp.int32)
        ids = [jnp.zeros((ROWS - SUB, 4 * SUB), F32) for _ in range(GROUP // CAP)]
        for s in range(GROUP):
            which = blk[GROUP * group + s]
            b = jnp.maximum(which, 0)
            live = jnp.where(row == s, jnp.where(which < 0, 0, fill_ref[b]), live)
            local = (sub_ref[b] >> (tiles.bit_length() - 1)).astype(F32)
            ids[s // CAP] = jnp.where(lane16 // (2 * SUB) == s % CAP, local, ids[s // CAP])
            coord = coord_ref[b].astype(F32)
            uv[0, s : s + 1, :] = coord[:1]
            uv[1, s : s + 1, :] = coord[1:]
            volt[s * step : s * step + 2 * chans, :] = vis_ref[b].astype(F32)
        keep = lane < live
        steps = [uv[axis] * (math.pi / SUB) for axis in range(2)]
        def multiply(chunk, part, parts):
            at = slice(part * 2 * SUB * GROUP // parts, (part + 1) * 2 * SUB * GROUP // parts)
            made = lax.dot_general(
                bufs[2 * chunk][at, :], bufs[2 * chunk + 1][...], (((1,), (1,)), ((), ())), preferred_element_type=F32
            )
            if chunk == 0:
                acc[at, :] = made
            else:
                acc[at, :] += made

        PARTS = 2
        for chunk in range(len(bufs) // 2):
            left, right = bufs[2 * chunk : 2 * chunk + 2]
            for i in range(chans * 2 // len(bufs)):
                c = chunk * (chans * 2 // len(bufs)) + i
                at = slice(i * lanes, (i + 1) * lanes)
                (su, cu), (sv, cv) = [sincos(value * freq_ref[0, c], 5) for value in steps]
                turn_re = cu * cv - su * sv
                turn_im = su * cv + cu * sv
                w_re = jnp.where(keep, volt[pl.ds(c, GROUP, stride=step), :], 0.0)
                w_im = jnp.where(keep, volt[pl.ds(chans + c, GROUP, stride=step), :], 0.0)
                w = (w_re * turn_re + w_im * turn_im, w_im * turn_re - w_re * turn_im)
                for axis, (sine, cosine) in enumerate(((su, cu), (sv, cv))):
                    twice = 2.0 - 4.0 * sine * sine
                    now = (cosine, sine)
                    last = (cosine, -sine)
                    for h in range(0, HALF, 2):
                        after = tuple(twice * a - z for a, z in zip(now, last))
                        for trig in range(2):
                            both = (now[trig], after[trig])
                            n = trig * HALF + h
                            if axis == 0:
                                for part in range(2):
                                    r = (part * SUB + n) * GROUP
                                    left[r : r + 2 * GROUP, at] = jnp.concatenate(
                                        [w[part] * x for x in both], axis=0
                                    ).astype(BF16)
                            else:
                                right[n * GROUP : (n + 2) * GROUP, at] = jnp.concatenate(both, axis=0).astype(BF16)
                        now, last = tuple(twice * a - z for a, z in zip(after, now)), after
                if chunk > 0 and (i + 1) % ((chans * 2 // len(bufs)) // PARTS) == 0:
                    multiply(chunk - 1, i // ((chans * 2 // len(bufs)) // PARTS), PARTS)
        for part in range(PARTS):
            multiply(len(bufs) // 2 - 1, part, PARTS)
        own = jnp.where(same, acc[...], 0.0).astype(BF16)
        wide = jnp.dot(own[: SUB * GROUP], place[0], preferred_element_type=F32)
        wide += jnp.dot(own[SUB * GROUP :], place[1], preferred_element_type=F32)
        skies = jnp.dot(gather, wide.astype(BF16), preferred_element_type=F32).astype(BF16)
        for p in range(GROUP // CAP):
            out_ref[GROUP // CAP * group + p, :SUB, :] = skies[p * SUB : (p + 1) * SUB]
            out_ref[GROUP // CAP * group + p, SUB:, :] = ids[p].astype(BF16)


def form_skies(vis, coords, block_fill, block_sub, freq, tiles):
    blocks, parts, lanes = vis.shape
    chans = parts // 2
    chunks = 8
    hbm = pl.BlockSpec(memory_space=pltpu.HBM)
    vmem = pl.BlockSpec(memory_space=pltpu.VMEM)
    bufs = []
    for _ in range(chunks):
        bufs.append(pltpu.VMEM((2 * SUB * GROUP, chans // chunks * lanes), BF16))
        bufs.append(pltpu.VMEM((SUB * GROUP, chans // chunks * lanes), BF16))
    return pl.pallas_call(
        functools.partial(sky_kernel, tiles),
        in_specs=[hbm] * 5,
        out_specs=vmem,
        scratch_shapes=[
            pltpu.SMEM(block_sub.shape, jnp.int32),
            pltpu.SMEM(block_fill.shape, jnp.int32),
            pltpu.SMEM(freq.shape, F32),
            pltpu.VMEM(vis.shape, BF16),
            pltpu.VMEM(coords.shape, BF16),
            pltpu.SMEM((CAP * tiles,), jnp.int32),
            pltpu.SMEM((tiles,), jnp.int32),
            pltpu.SemaphoreType.DMA((5,)),
            pltpu.VMEM((GROUP * (parts + 1) + 7, lanes), F32),
            pltpu.VMEM((2, GROUP, lanes), F32),
            pltpu.VMEM((2 * SUB * GROUP, SUB * GROUP), F32),
        ] + bufs,
        out_shape=jax.ShapeDtypeStruct((tiles, ROWS, 4 * SUB), BF16),
        compiler_params=pltpu.CompilerParams(vmem_limit_bytes=LIMIT),
        name="skies",
    )(block_sub, block_fill, freq, vis, coords)


def sum_kernel(got_ref, fold_ref, phase_ref, out_ref, acc):
    tiles = got_ref.shape[0]
    acc[...] = jnp.zeros_like(acc)
    for sender in range(tiles):
        data = got_ref[sender, :SUB, :].astype(F32)
        ids = got_ref[sender, SUB:, :].astype(F32)[:1]
        for sub in range(SPP):
            at = slice(sub // 2 * SUB, (sub // 2 + 1) * SUB)
            lanes = slice(sub % 2 * 4 * SUB, (sub % 2 + 1) * 4 * SUB)
            acc[at, lanes] += jnp.where(ids == sub, data, 0.0)
    made = lax.dot_general(
        acc[...], fold_ref[...], (((1,), (0,)), ((), ())),
        precision=lax.Precision.HIGHEST, preferred_element_type=F32,
    )
    turned = pltpu.roll(made, 2 * SUB, 1)
    for pair in range(SPP // 2):
        at = slice(pair * SUB, (pair + 1) * SUB)
        other = SPP // 2 + pair
        value = made[at] * phase_ref[pair : pair + 1] + turned[at] * phase_ref[other : other + 1]
        value = value.astype(BF16)
        half = pair // (SPP // 4)
        at = slice(pair % (SPP // 4) * SUB, (pair % (SPP // 4) + 1) * SUB)
        for target in range(half, tiles, 2):
            out_ref[target, at, :] = value


def sum_subgrids(got, phase):
    vmem = pl.BlockSpec(memory_space=pltpu.VMEM)
    return pl.pallas_call(
        sum_kernel,
        in_specs=[vmem] * 3,
        out_specs=vmem,
        out_shape=jax.ShapeDtypeStruct((got.shape[0], SPP // 4 * SUB, 4 * SUB), BF16),
        scratch_shapes=[pltpu.VMEM((SPP // 2 * SUB, 8 * SUB), F32)],
        compiler_params=pltpu.CompilerParams(vmem_limit_bytes=LIMIT),
        name="sums",
    )(got, jnp.asarray(fold_matrix()), phase)


def column_phases(norm, tiles, me, pos_ref, plane_ref, w_ref, phase_ref):
    lane = lax.broadcasted_iota(jnp.int32, (SPP, 4 * SUB), 1)
    row = lax.broadcasted_iota(jnp.int32, (SPP, 4 * SUB), 0)
    column = lane % SUB
    odd = lane // SUB % 2
    first = jnp.zeros((SPP, 4 * SUB), jnp.int32)
    w = jnp.zeros((SPP, 4 * SUB), F32)
    for sub in range(SPP):
        here = (row % (SPP // 2) == sub // 2) & (odd == sub % 2)
        s = sub * tiles + me
        first = jnp.where(here, pos_ref[s, 1], first)
        w = jnp.where(here, w_ref[0, plane_ref[s]], w)
    x = (first + column).astype(F32) / NCOL - 0.5
    turns = w * (x * x) - ((31 * column) & 63).astype(F32) / 64
    c_re, c_im = cis(turns - jnp.round(turns))
    c_im = jnp.where(lane < 2 * SUB, -c_im, c_im)
    phase_ref[...] = jnp.where(row < SPP // 2, c_re, c_im) * norm


def phase_kernel(norm, tiles, me_ref, pos_ref, plane_ref, w_ref, mat_ref, turn_ref, base_ref, phase_ref):
    subs, rows = turn_ref.shape[1:]
    column_phases(norm, tiles, me_ref[0], pos_ref, plane_ref, w_ref, phase_ref)
    first = me_ref[0] * rows
    for k in range(subs):
        s = k % SPP * tiles + k // SPP
        turn_ref[0, k : k + 1, :] = jnp.full((1, rows), pos_ref[s, 0].astype(F32))
        turn_ref[1, k : k + 1, :] = jnp.full((1, rows), w_ref[0, plane_ref[s]])
    gy = turn_ref[0].astype(jnp.int32)
    q = first + lax.broadcasted_iota(jnp.int32, (subs, rows), 1)
    steps = (q * gy + NV // 2) & (NV - 1)
    pos = q.astype(F32) / NV - 0.5
    turns = (NV // 2 - steps).astype(F32) / NV + turn_ref[1] * (pos * pos)
    turn_ref[0], turn_ref[1] = cis(turns - jnp.round(turns))
    q = first + lax.broadcasted_iota(jnp.int32, (SUB, rows), 1)
    r = lax.broadcasted_iota(jnp.int32, (SUB, rows), 0)
    steps = ((q + 31 * NV // 64) * r + NV // 2) & (NV - 1)
    for part, value in enumerate(cis((NV // 2 - steps).astype(F32) / NV)):
        base_ref[part] = lax.dot_general(
            mat_ref[...], value, (((1,), (0,)), ((), ())),
            precision=lax.Precision.HIGHEST, preferred_element_type=F32,
        )


def make_phases(me, sub_pos, sub_plane, w_band, norm, tiles):
    rows = NV // tiles
    subs = sub_pos.shape[0]
    smem = pl.BlockSpec(memory_space=pltpu.SMEM)
    vmem = pl.BlockSpec(memory_space=pltpu.VMEM)
    return pl.pallas_call(
        functools.partial(phase_kernel, norm, tiles),
        in_specs=[smem] * 4 + [vmem],
        out_specs=[vmem] * 3,
        out_shape=[
            jax.ShapeDtypeStruct((2, subs, rows), F32),
            jax.ShapeDtypeStruct((2, SUB, rows), F32),
            jax.ShapeDtypeStruct((SPP, 4 * SUB), F32),
        ],
        compiler_params=pltpu.CompilerParams(vmem_limit_bytes=LIMIT),
        name="phases",
    )(me, sub_pos, sub_plane, w_band, jnp.asarray(column_matrix().T, F32))


def image_kernel(tiles, pos_ref, me_ref, turn_ref, base_ref, own_ref, other_ref, out_ref, acc, canvas, table):
    rows = out_ref.shape[0]
    second = me_ref[0] & 1
    lane = lax.broadcasted_iota(jnp.int32, (SUB, 4 * SUB), 1)
    base_re, base_im = base_ref[0], base_ref[1]
    acc[...] = jnp.zeros_like(acc)

    @pl.loop(0, tiles, unroll=8)
    def _(panel):
        for pair in range(SPP // 2):
            half = pair // (SPP // 4)
            at = slice(pair % (SPP // 4) * SUB, (pair % (SPP // 4) + 1) * SUB)
            z = jnp.where(second == half, own_ref[panel, at, :].astype(F32), other_ref[panel, at, :].astype(F32))
            for odd in range(2):
                sub = 2 * pair + odd
                first = pos_ref[sub * tiles + panel, 1]
                moved = pltpu.roll(z, (first - odd * SUB + 4 * SUB) & (4 * SUB - 1), 1)
                place = (lane & (NCOL - 1)) - first
                canvas[sub * SUB : (sub + 1) * SUB, :] = jnp.where((place >= 0) & (place < SUB), moved, 0.0)
        turn_re = turn_ref[0, pl.ds(panel * SPP, SPP), :]
        turn_im = turn_ref[1, pl.ds(panel * SPP, SPP), :]
        for sub in range(SPP):
            at = slice(sub * SUB, (sub + 1) * SUB)
            t_re, t_im = turn_re[sub : sub + 1], turn_im[sub : sub + 1]
            table[at, :rows] = (t_re * base_re - t_im * base_im).astype(BF16)
            table[at, rows:] = (t_re * base_im + t_im * base_re).astype(BF16)
        acc[...] += jnp.dot(canvas[...].T.astype(BF16), table[...], preferred_element_type=F32)

    real = acc[:NCOL, :rows] - acc[NCOL:, rows:]
    imag = acc[NCOL:, :rows] + acc[:NCOL, rows:]
    out_ref[...] = jnp.concatenate([real, imag], axis=0).T


def make_image(turn, base, own, other, sub_pos, me):
    tiles = own.shape[0]
    rows = turn.shape[2]
    smem = pl.BlockSpec(memory_space=pltpu.SMEM)
    vmem = pl.BlockSpec(memory_space=pltpu.VMEM)
    return pl.pallas_call(
        functools.partial(image_kernel, tiles),
        in_specs=[smem] * 2 + [vmem] * 4,
        out_specs=vmem,
        out_shape=jax.ShapeDtypeStruct((rows, 4 * SUB), F32),
        scratch_shapes=[
            pltpu.VMEM((4 * SUB, 2 * rows), F32),
            pltpu.VMEM((SPP * SUB, 4 * SUB), F32),
            pltpu.VMEM((SPP * SUB, 2 * rows), BF16),
        ],
        compiler_params=pltpu.CompilerParams(vmem_limit_bytes=LIMIT),
        name="image",
    )(sub_pos, me, turn, base, own, other)


def shards(vis, coords, block_fill, block_sub, sub_pos, sub_plane, freq, plane_w):
    tiles = lax.axis_size("tile")
    me = lax.axis_index("tile").reshape(1)
    norm = 1.0 / (math.sqrt(vis.shape[2] // 2 * vis.shape[3]) * SUB * math.sqrt(NV))
    skies = form_skies(vis[0], coords, block_fill, block_sub, freq, tiles)
    turn, base, phase = make_phases(me, sub_pos, sub_plane, plane_w, norm, tiles)
    got = lax.all_to_all(skies, "tile", split_axis=0, concat_axis=0, tiled=True)
    halves = sum_subgrids(got, phase)
    own = lax.all_to_all(halves, "tile", split_axis=0, concat_axis=0, tiled=True)
    other = lax.ppermute(own, "tile", [(i, i ^ 1) for i in range(tiles)])
    return make_image(turn, base, own, other, sub_pos, me)[None]


def solution(mesh):
    return jax.shard_map(
        shards,
        mesh=mesh,
        in_specs=(
            P("band", "tile", None, None),
            P("tile", None, None),
            P("tile"),
            P("tile"),
            P(),
            P(),
            P("band", None),
            P("band", None),
        ),
        out_specs=P("band", "tile", None),
        check_vma=False,
    )
```

```python
import functools
import math

import jax
import jax.numpy as jnp
import numpy as np
from jax import lax
from jax.experimental import pallas as pl
from jax.experimental.pallas import tpu as pltpu
from jax.sharding import PartitionSpec as P

SUB = 32
HALF = SUB // 2
CAP = 2
NV = 8192
NCOL = 64
SPP = 8
ROWS = 48
GROUP = 8
LIMIT = 60 * 2**20
SMALL = 16 * 2**20
F32 = jnp.float32
BF16 = jnp.bfloat16


def poly(x2, coefs):
    acc = jnp.full_like(x2, coefs[-1])
    for coef in coefs[-2::-1]:
        acc = acc * x2 + coef
    return acc


def sincos(x, terms):
    x2 = x * x
    sine = x * poly(x2, [(-1.0) ** k / math.factorial(2 * k + 1) for k in range(terms)])
    cosine = poly(x2, [(-1.0) ** k / math.factorial(2 * k) for k in range(terms + 1)])
    return sine, cosine


def cis(turns):
    sine, cosine = sincos(turns * math.pi, 6)
    return 1.0 - 2.0 * sine * sine, 2.0 * sine * cosine


def column_matrix():
    p = np.arange(SUB)[:, None]
    h = np.arange(HALF)[None, :]
    taper = 1.0 - 0.9 * ((2 * h + 1) / SUB) ** 2
    angle = 2.0 * np.pi * p * (h + 0.5) / SUB
    return np.concatenate([2 * taper * np.cos(angle), 2 * taper * np.sin(angle)], axis=1)


def pick_matrices():
    iota = lambda shape, dim: lax.broadcasted_iota(jnp.int32, shape, dim)
    one = lambda mask: jnp.where(mask, 1.0, 0.0).astype(BF16)
    shape = (SUB * GROUP, 4 * SUB)
    k, lane = iota(shape, 0), iota(shape, 1)
    fits = (k // GROUP == lane % SUB) & (k % CAP == lane // (2 * SUB))
    place = [one(fits & (lane // SUB % 2 == part)) for part in range(2)]
    shape = (GROUP // CAP * SUB, SUB * GROUP)
    r, k = iota(shape, 0), iota(shape, 1)
    return place, one((r % SUB == k // GROUP) & (r // SUB == k % GROUP // CAP))


def sky_kernel(tiles, sub_hbm, fill_hbm, freq_hbm, vis_hbm, coord_hbm, out_ref,
               sub_ref, fill_ref, freq_ref, vis_ref, coord_ref, blk, count, sems, volt, uv, acc, *bufs):
    blocks = vis_ref.shape[0]
    chans = vis_ref.shape[1] // 2
    lanes = vis_ref.shape[2]
    step = 2 * chans + 1
    pairs = ((sub_hbm, sub_ref), (fill_hbm, fill_ref), (freq_hbm, freq_ref), (coord_hbm, coord_ref), (vis_hbm, vis_ref))
    copies = [pltpu.make_async_copy(a, b, sems.at[i]) for i, (a, b) in enumerate(pairs)]
    for copy in copies:
        copy.start()

    @pl.loop(0, tiles)
    def _(i):
        count[i] = 0
        for j in range(CAP):
            blk[CAP * i + j] = -1

    for copy in copies:
        copy.wait()

    @pl.loop(0, blocks)
    def _(b):
        p = sub_ref[b] & (tiles - 1)
        have = count[p]
        blk[CAP * p + have] = b
        count[p] = have + 1

    place, gather = pick_matrices()
    lane = lax.broadcasted_iota(jnp.int32, (GROUP, lanes), 1)
    row = lax.broadcasted_iota(jnp.int32, (GROUP, lanes), 0)
    lane16 = lax.broadcasted_iota(jnp.int32, (ROWS - SUB, 4 * SUB), 1)
    same = (lax.broadcasted_iota(jnp.int32, (2 * SUB * GROUP, SUB * GROUP), 0) % GROUP
            == lax.broadcasted_iota(jnp.int32, (2 * SUB * GROUP, SUB * GROUP), 1) % GROUP)

    @pl.loop(0, CAP * tiles // GROUP)
    def _(group):
        live = jnp.zeros((GROUP, lanes), jnp.int32)
        ids = [jnp.zeros((ROWS - SUB, 4 * SUB), F32) for _ in range(GROUP // CAP)]
        for s in range(GROUP):
            which = blk[GROUP * group + s]
            b = jnp.maximum(which, 0)
            live = jnp.where(row == s, jnp.where(which < 0, 0, fill_ref[b]), live)
            local = (sub_ref[b] >> (tiles.bit_length() - 1)).astype(F32)
            ids[s // CAP] = jnp.where(lane16 // (2 * SUB) == s % CAP, local, ids[s // CAP])
            coord = coord_ref[b].astype(F32)
            uv[0, s : s + 1, :] = coord[:1]
            uv[1, s : s + 1, :] = coord[1:]
            volt[s * step : s * step + 2 * chans, :] = vis_ref[b].astype(F32)
        keep = lane < live
        steps = [uv[axis] * (math.pi / SUB) for axis in range(2)]
        def multiply(chunk, part, parts):
            at = slice(part * 2 * SUB * GROUP // parts, (part + 1) * 2 * SUB * GROUP // parts)
            made = lax.dot_general(
                bufs[2 * chunk][at, :], bufs[2 * chunk + 1][...], (((1,), (1,)), ((), ())), preferred_element_type=F32
            )
            if chunk == 0:
                acc[at, :] = made
            else:
                acc[at, :] += made

        PARTS = 2
        for chunk in range(len(bufs) // 2):
            left, right = bufs[2 * chunk : 2 * chunk + 2]
            for i in range(chans * 2 // len(bufs)):
                c = chunk * (chans * 2 // len(bufs)) + i
                at = slice(i * lanes, (i + 1) * lanes)
                (su, cu), (sv, cv) = [sincos(value * freq_ref[0, c], 5) for value in steps]
                turn_re = cu * cv - su * sv
                turn_im = su * cv + cu * sv
                w_re = jnp.where(keep, volt[pl.ds(c, GROUP, stride=step), :], 0.0)
                w_im = jnp.where(keep, volt[pl.ds(chans + c, GROUP, stride=step), :], 0.0)
                w = (w_re * turn_re + w_im * turn_im, w_im * turn_re - w_re * turn_im)
                for axis, (sine, cosine) in enumerate(((su, cu), (sv, cv))):
                    twice = 2.0 - 4.0 * sine * sine
                    now = (cosine, sine)
                    last = (cosine, -sine)
                    for h in range(0, HALF, 2):
                        after = tuple(twice * a - z for a, z in zip(now, last))
                        for trig in range(2):
                            both = (now[trig], after[trig])
                            n = trig * HALF + h
                            if axis == 0:
                                for part in range(2):
                                    r = (part * SUB + n) * GROUP
                                    left[r : r + 2 * GROUP, at] = jnp.concatenate(
                                        [w[part] * x for x in both], axis=0
                                    ).astype(BF16)
                            else:
                                right[n * GROUP : (n + 2) * GROUP, at] = jnp.concatenate(both, axis=0).astype(BF16)
                        now, last = tuple(twice * a - z for a, z in zip(after, now)), after
                if chunk > 0 and (i + 1) % ((chans * 2 // len(bufs)) // PARTS) == 0:
                    multiply(chunk - 1, i // ((chans * 2 // len(bufs)) // PARTS), PARTS)
        for part in range(PARTS):
            multiply(len(bufs) // 2 - 1, part, PARTS)
        own = jnp.where(same, acc[...], 0.0).astype(BF16)
        wide = jnp.dot(own[: SUB * GROUP], place[0], preferred_element_type=F32)
        wide += jnp.dot(own[SUB * GROUP :], place[1], preferred_element_type=F32)
        skies = jnp.dot(gather, wide.astype(BF16), preferred_element_type=F32).astype(BF16)
        for p in range(GROUP // CAP):
            out_ref[GROUP // CAP * group + p, :SUB, :] = skies[p * SUB : (p + 1) * SUB]
            out_ref[GROUP // CAP * group + p, SUB:, :] = ids[p].astype(BF16)


def form_skies(vis, coords, block_fill, block_sub, freq, tiles):
    blocks, parts, lanes = vis.shape
    chans = parts // 2
    chunks = 8
    hbm = pl.BlockSpec(memory_space=pltpu.HBM)
    vmem = pl.BlockSpec(memory_space=pltpu.VMEM)
    bufs = []
    for _ in range(chunks):
        bufs.append(pltpu.VMEM((2 * SUB * GROUP, chans // chunks * lanes), BF16))
        bufs.append(pltpu.VMEM((SUB * GROUP, chans // chunks * lanes), BF16))
    return pl.pallas_call(
        functools.partial(sky_kernel, tiles),
        in_specs=[hbm] * 5,
        out_specs=vmem,
        scratch_shapes=[
            pltpu.SMEM(block_sub.shape, jnp.int32),
            pltpu.SMEM(block_fill.shape, jnp.int32),
            pltpu.SMEM(freq.shape, F32),
            pltpu.VMEM(vis.shape, BF16),
            pltpu.VMEM(coords.shape, BF16),
            pltpu.SMEM((CAP * tiles,), jnp.int32),
            pltpu.SMEM((tiles,), jnp.int32),
            pltpu.SemaphoreType.DMA((5,)),
            pltpu.VMEM((GROUP * (parts + 1) + 7, lanes), F32),
            pltpu.VMEM((2, GROUP, lanes), F32),
            pltpu.VMEM((2 * SUB * GROUP, SUB * GROUP), F32),
        ] + bufs,
        out_shape=jax.ShapeDtypeStruct((tiles, ROWS, 4 * SUB), BF16),
        compiler_params=pltpu.CompilerParams(vmem_limit_bytes=LIMIT),
        name="skies",
    )(block_sub, block_fill, freq, vis, coords)


def fold_matrix():
    shape = (8 * SUB, 4 * SUB)
    row, lane = lax.broadcasted_iota(jnp.int32, shape, 0), lax.broadcasted_iota(jnp.int32, shape, 1)
    h, p = row % HALF, lane % SUB
    taper = (2 * h + 1).astype(F32) / SUB
    taper = 2.0 - 1.8 * taper * taper
    turns = ((p * (2 * h + 1) + 32) & 63) - 32
    cosine, sine = cis(turns.astype(F32) / 64)
    fits = (row // (4 * SUB) == lane // SUB % 2) & (row // SUB % 2 == lane // (2 * SUB))
    return jnp.where(fits, taper * jnp.where(row % SUB < HALF, cosine, sine), 0.0)


def sum_kernel(got_ref, phase_ref, out_ref, acc):
    tiles = got_ref.shape[0]
    acc[...] = jnp.zeros_like(acc)
    for sender in range(tiles):
        data = got_ref[sender, :SUB, :].astype(F32)
        ids = got_ref[sender, SUB:, :].astype(F32)[:1]
        for sub in range(SPP):
            at = slice(sub // 2 * SUB, (sub // 2 + 1) * SUB)
            lanes = slice(sub % 2 * 4 * SUB, (sub % 2 + 1) * 4 * SUB)
            acc[at, lanes] += jnp.where(ids == sub, data, 0.0)
    made = lax.dot_general(
        acc[...], fold_matrix(), (((1,), (0,)), ((), ())),
        precision=lax.Precision.HIGHEST, preferred_element_type=F32,
    )
    turned = pltpu.roll(made, 2 * SUB, 1)
    for pair in range(SPP // 2):
        at = slice(pair * SUB, (pair + 1) * SUB)
        other = SPP // 2 + pair
        out_ref[at, :] = (made[at] * phase_ref[pair : pair + 1] + turned[at] * phase_ref[other : other + 1]).astype(BF16)


def sum_subgrids(got, phase):
    vmem = pl.BlockSpec(memory_space=pltpu.VMEM)
    return pl.pallas_call(
        sum_kernel,
        in_specs=[vmem] * 2,
        out_specs=vmem,
        out_shape=jax.ShapeDtypeStruct((SPP // 2 * SUB, 4 * SUB), BF16),
        scratch_shapes=[pltpu.VMEM((SPP // 2 * SUB, 8 * SUB), F32)],
        compiler_params=pltpu.CompilerParams(vmem_limit_bytes=SMALL),
        name="sums",
    )(got, phase)


def column_phases(norm, tiles, me, pos_ref, plane_ref, w_ref, phase_ref):
    lane = lax.broadcasted_iota(jnp.int32, (SPP, 4 * SUB), 1)
    row = lax.broadcasted_iota(jnp.int32, (SPP, 4 * SUB), 0)
    column = lane % SUB
    odd = lane // SUB % 2
    first = jnp.zeros((SPP, 4 * SUB), jnp.int32)
    w = jnp.zeros((SPP, 4 * SUB), F32)
    for sub in range(SPP):
        here = (row % (SPP // 2) == sub // 2) & (odd == sub % 2)
        s = sub * tiles + me
        first = jnp.where(here, pos_ref[s, 1], first)
        w = jnp.where(here, w_ref[0, plane_ref[s]], w)
    x = (first + column).astype(F32) / NCOL - 0.5
    turns = w * (x * x) - ((31 * column) & 63).astype(F32) / 64
    c_re, c_im = cis(turns - jnp.round(turns))
    c_im = jnp.where(lane < 2 * SUB, -c_im, c_im)
    phase_ref[...] = jnp.where(row < SPP // 2, c_re, c_im) * norm


def phase_kernel(norm, tiles, me_ref, pos_ref, plane_ref, w_ref, mat_ref, turn_ref, base_ref, phase_ref):
    subs, rows = turn_ref.shape[1:]
    column_phases(norm, tiles, me_ref[0], pos_ref, plane_ref, w_ref, phase_ref)
    first = me_ref[0] * rows
    for k in range(subs):
        s = k % SPP * tiles + k // SPP
        turn_ref[0, k : k + 1, :] = jnp.full((1, rows), pos_ref[s, 0].astype(F32))
        turn_ref[1, k : k + 1, :] = jnp.full((1, rows), w_ref[0, plane_ref[s]])
    gy = turn_ref[0].astype(jnp.int32)
    q = first + lax.broadcasted_iota(jnp.int32, (subs, rows), 1)
    steps = (q * gy + NV // 2) & (NV - 1)
    pos = q.astype(F32) / NV - 0.5
    turns = (NV // 2 - steps).astype(F32) / NV + turn_ref[1] * (pos * pos)
    turn_ref[0], turn_ref[1] = cis(turns - jnp.round(turns))
    q = first + lax.broadcasted_iota(jnp.int32, (SUB, rows), 1)
    r = lax.broadcasted_iota(jnp.int32, (SUB, rows), 0)
    steps = ((q + 31 * NV // 64) * r + NV // 2) & (NV - 1)
    for part, value in enumerate(cis((NV // 2 - steps).astype(F32) / NV)):
        base_ref[part] = lax.dot_general(
            mat_ref[...], value, (((1,), (0,)), ((), ())),
            precision=lax.Precision.HIGHEST, preferred_element_type=F32,
        )


def make_phases(me, sub_pos, sub_plane, w_band, norm, tiles):
    rows = NV // tiles
    subs = sub_pos.shape[0]
    smem = pl.BlockSpec(memory_space=pltpu.SMEM)
    vmem = pl.BlockSpec(memory_space=pltpu.VMEM)
    return pl.pallas_call(
        functools.partial(phase_kernel, norm, tiles),
        in_specs=[smem] * 4 + [vmem],
        out_specs=[vmem] * 3,
        out_shape=[
            jax.ShapeDtypeStruct((2, subs, rows), F32),
            jax.ShapeDtypeStruct((2, SUB, rows), F32),
            jax.ShapeDtypeStruct((SPP, 4 * SUB), F32),
        ],
        compiler_params=pltpu.CompilerParams(vmem_limit_bytes=LIMIT),
        name="phases",
    )(me, sub_pos, sub_plane, w_band, jnp.asarray(column_matrix().T, F32))


def image_kernel(tiles, sides, first_part, last_part, pos_ref, me_ref, turn_ref, base_ref, *refs):
    zs, refs = refs[: len(sides)], refs[len(sides) :]
    start = None
    if not first_part:
        start, refs = refs[0], refs[1:]
    out_ref, refs = refs[0], refs[1:]
    acc = out_ref
    if last_part:
        acc, refs = refs[0], refs[1:]
    canvas, table = refs
    rows = turn_ref.shape[2]
    me = me_ref[0]
    depth = tiles // 4
    lane = lax.broadcasted_iota(jnp.int32, (SUB, 4 * SUB), 1)
    base_re, base_im = base_ref[0], base_ref[1]
    acc[...] = jnp.zeros(acc.shape, F32) if first_part else start[...]
    for side, z_ref in zip(sides, zs):

        @pl.loop(0, depth, unroll=4)
        def _(t):
            panel = ((me // 4 - t) & (depth - 1)) * 4 + ((me & 3) ^ side)
            for pair in range(SPP // 2):
                z = z_ref[t, pair * SUB : (pair + 1) * SUB, :].astype(F32)
                for odd in range(2):
                    sub = 2 * pair + odd
                    first = pos_ref[sub * tiles + panel, 1]
                    moved = pltpu.roll(z, (first - odd * SUB + 4 * SUB) & (4 * SUB - 1), 1)
                    place = (lane & (NCOL - 1)) - first
                    canvas[sub * SUB : (sub + 1) * SUB, :] = jnp.where((place >= 0) & (place < SUB), moved, 0.0)
            turn_re = turn_ref[0, pl.ds(panel * SPP, SPP), :]
            turn_im = turn_ref[1, pl.ds(panel * SPP, SPP), :]
            for sub in range(SPP):
                at = slice(sub * SUB, (sub + 1) * SUB)
                t_re, t_im = turn_re[sub : sub + 1], turn_im[sub : sub + 1]
                table[at, :rows] = (t_re * base_re - t_im * base_im).astype(BF16)
                table[at, rows:] = (t_re * base_im + t_im * base_re).astype(BF16)
            acc[...] += jnp.dot(canvas[...].T.astype(BF16), table[...], preferred_element_type=F32)

    if last_part:
        real = acc[:NCOL, :rows] - acc[NCOL:, rows:]
        imag = acc[NCOL:, :rows] + acc[:NCOL, rows:]
        out_ref[...] = jnp.concatenate([real, imag], axis=0).T


def make_image(turn, base, zs, sides, sub_pos, me, tiles, start=None, last=False):
    rows = turn.shape[2]
    smem = pl.BlockSpec(memory_space=pltpu.SMEM)
    vmem = pl.BlockSpec(memory_space=pltpu.VMEM)
    carry = [] if start is None else [start]
    scratch = [
        pltpu.VMEM((4 * SUB, 2 * rows), F32),
        pltpu.VMEM((SPP * SUB, 4 * SUB), F32),
        pltpu.VMEM((SPP * SUB, 2 * rows), BF16),
    ]
    return pl.pallas_call(
        functools.partial(image_kernel, tiles, sides, start is None, last),
        in_specs=[smem] * 2 + [vmem] * (2 + len(zs) + len(carry)),
        out_specs=vmem,
        out_shape=jax.ShapeDtypeStruct((rows, 4 * SUB) if last else (4 * SUB, 2 * rows), F32),
        scratch_shapes=scratch if last else scratch[1:],
        compiler_params=pltpu.CompilerParams(vmem_limit_bytes=SMALL),
        name="image",
    )(sub_pos, me, turn, base, *zs, *carry)


def shards(vis, coords, block_fill, block_sub, sub_pos, sub_plane, freq, plane_w):
    tiles = lax.axis_size("tile")
    me = lax.axis_index("tile").reshape(1)
    norm = 1.0 / (math.sqrt(vis.shape[2] // 2 * vis.shape[3]) * SUB * math.sqrt(NV))
    skies = form_skies(vis[0], coords, block_fill, block_sub, freq, tiles)
    turn, base, phase = make_phases(me, sub_pos, sub_plane, plane_w, norm, tiles)
    got = lax.all_to_all(skies, "tile", split_axis=0, concat_axis=0, tiled=True)
    z = sum_subgrids(got, phase)
    depth = tiles // 4
    ahead = lambda i, t: (i // 4 + t) % depth * 4 + i % 4
    column = [z] + [lax.ppermute(z, "tile", [(i, ahead(i, t)) for i in range(tiles)]) for t in range(1, depth)]
    column = jnp.stack(column)
    beside = [(i, i ^ 1) for i in range(tiles)]
    across = lax.ppermute(column, "tile", [(i, i ^ 2) for i in range(tiles)])
    twin = lax.ppermute(column, "tile", beside)
    part = make_image(turn, base, [column, twin], [0, 1], sub_pos, me, tiles)
    across, part = lax.optimization_barrier((across, part))
    far = lax.ppermute(across, "tile", beside)
    return make_image(turn, base, [across, far], [2, 3], sub_pos, me, tiles, part, True)[None]


def solution(mesh):
    return jax.shard_map(
        shards,
        mesh=mesh,
        in_specs=(
            P("band", "tile", None, None),
            P("tile", None, None),
            P("tile"),
            P("tile"),
            P(),
            P(),
            P("band", None),
            P("band", None),
        ),
        out_specs=P("band", "tile", None),
        check_vma=False,
    )
```

```python
import functools
import math

import jax
import jax.numpy as jnp
import numpy as np
from jax import lax
from jax.experimental import pallas as pl
from jax.experimental.pallas import tpu as pltpu
from jax.sharding import PartitionSpec as P

SUB = 32
HALF = SUB // 2
CAP = 2
NV = 8192
NCOL = 64
SPP = 8
ROWS = 40
GROUP = 8
LIMIT = 60 * 2**20
SMALL = 16 * 2**20
F32 = jnp.float32
BF16 = jnp.bfloat16


def poly(x2, coefs):
    acc = jnp.full_like(x2, coefs[-1])
    for coef in coefs[-2::-1]:
        acc = acc * x2 + coef
    return acc


def sincos(x, terms):
    x2 = x * x
    sine = x * poly(x2, [(-1.0) ** k / math.factorial(2 * k + 1) for k in range(terms)])
    cosine = poly(x2, [(-1.0) ** k / math.factorial(2 * k) for k in range(terms + 1)])
    return sine, cosine


def cis(turns):
    sine, cosine = sincos(turns * math.pi, 6)
    return 1.0 - 2.0 * sine * sine, 2.0 * sine * cosine


def column_matrix():
    p = np.arange(SUB)[:, None]
    h = np.arange(HALF)[None, :]
    taper = 1.0 - 0.9 * ((2 * h + 1) / SUB) ** 2
    angle = 2.0 * np.pi * p * (h + 0.5) / SUB
    return np.concatenate([2 * taper * np.cos(angle), 2 * taper * np.sin(angle)], axis=1)


def pick_matrices():
    iota = lambda shape, dim: lax.broadcasted_iota(jnp.int32, shape, dim)
    one = lambda mask: jnp.where(mask, 1.0, 0.0).astype(BF16)
    shape = (SUB * GROUP, 4 * SUB)
    k, lane = iota(shape, 0), iota(shape, 1)
    fits = (k // GROUP == lane % SUB) & (k % CAP == lane // (2 * SUB))
    place = [one(fits & (lane // SUB % 2 == part)) for part in range(2)]
    shape = (GROUP // CAP * SUB, SUB * GROUP)
    r, k = iota(shape, 0), iota(shape, 1)
    return place, one((r % SUB == k // GROUP) & (r // SUB == k % GROUP // CAP))


def sky_kernel(tiles, sub_hbm, fill_hbm, freq_hbm, vis_hbm, coord_hbm, out_ref,
               sub_ref, fill_ref, freq_ref, vis_ref, coord_ref, blk, count, sems, volt, uv, acc, *bufs):
    blocks = vis_ref.shape[0]
    chans = vis_ref.shape[1] // 2
    lanes = vis_ref.shape[2]
    step = 2 * chans + 1
    pairs = ((sub_hbm, sub_ref), (fill_hbm, fill_ref), (freq_hbm, freq_ref), (coord_hbm, coord_ref), (vis_hbm, vis_ref))
    copies = [pltpu.make_async_copy(a, b, sems.at[i]) for i, (a, b) in enumerate(pairs)]
    for copy in copies:
        copy.start()

    @pl.loop(0, tiles)
    def _(i):
        count[i] = 0
        for j in range(CAP):
            blk[CAP * i + j] = -1

    for copy in copies[:2]:
        copy.wait()

    @pl.loop(0, blocks)
    def _(b):
        p = sub_ref[b] & (tiles - 1)
        have = count[p]
        blk[CAP * p + have] = b
        count[p] = have + 1

    for copy in copies[2:]:
        copy.wait()

    place, gather = pick_matrices()
    lane = lax.broadcasted_iota(jnp.int32, (GROUP, lanes), 1)
    row = lax.broadcasted_iota(jnp.int32, (GROUP, lanes), 0)
    lane16 = lax.broadcasted_iota(jnp.int32, (ROWS - SUB, 4 * SUB), 1)
    same = (lax.broadcasted_iota(jnp.int32, (2 * SUB * GROUP, SUB * GROUP), 0) % GROUP
            == lax.broadcasted_iota(jnp.int32, (2 * SUB * GROUP, SUB * GROUP), 1) % GROUP)

    @pl.loop(0, CAP * tiles // GROUP)
    def _(group):
        live = jnp.zeros((GROUP, lanes), jnp.int32)
        ids = [jnp.zeros((ROWS - SUB, 4 * SUB), F32) for _ in range(GROUP // CAP)]
        for s in range(GROUP):
            which = blk[GROUP * group + s]
            b = jnp.maximum(which, 0)
            live = jnp.where(row == s, jnp.where(which < 0, 0, fill_ref[b]), live)
            local = (sub_ref[b] >> (tiles.bit_length() - 1)).astype(F32)
            ids[s // CAP] = jnp.where(lane16 // (2 * SUB) == s % CAP, local, ids[s // CAP])
            coord = coord_ref[b].astype(F32)
            uv[0, s : s + 1, :] = coord[:1]
            uv[1, s : s + 1, :] = coord[1:]
            volt[s * step : s * step + 2 * chans, :] = vis_ref[b].astype(F32)
        keep = lane < live
        steps = [uv[axis] * (math.pi / SUB) for axis in range(2)]
        def multiply(chunk, part, parts):
            at = slice(part * 2 * SUB * GROUP // parts, (part + 1) * 2 * SUB * GROUP // parts)
            made = lax.dot_general(
                bufs[2 * chunk][at, :], bufs[2 * chunk + 1][...], (((1,), (1,)), ((), ())), preferred_element_type=F32
            )
            if chunk == 0:
                acc[at, :] = made
            else:
                acc[at, :] += made

        PARTS = 2
        for chunk in range(len(bufs) // 2):
            left, right = bufs[2 * chunk : 2 * chunk + 2]
            for i in range(chans * 2 // len(bufs)):
                c = chunk * (chans * 2 // len(bufs)) + i
                at = slice(i * lanes, (i + 1) * lanes)
                (su, cu), (sv, cv) = [sincos(value * freq_ref[0, c], 5) for value in steps]
                turn_re = cu * cv - su * sv
                turn_im = su * cv + cu * sv
                w_re = jnp.where(keep, volt[pl.ds(c, GROUP, stride=step), :], 0.0)
                w_im = jnp.where(keep, volt[pl.ds(chans + c, GROUP, stride=step), :], 0.0)
                w = (w_re * turn_re + w_im * turn_im, w_im * turn_re - w_re * turn_im)
                for axis, (sine, cosine) in enumerate(((su, cu), (sv, cv))):
                    twice = 2.0 - 4.0 * sine * sine
                    now = (cosine, sine)
                    last = (cosine, -sine)
                    for h in range(0, HALF, 2):
                        after = tuple(twice * a - z for a, z in zip(now, last))
                        for trig in range(2):
                            both = (now[trig], after[trig])
                            n = trig * HALF + h
                            if axis == 0:
                                for part in range(2):
                                    r = (part * SUB + n) * GROUP
                                    left[r : r + 2 * GROUP, at] = jnp.concatenate(
                                        [w[part] * x for x in both], axis=0
                                    ).astype(BF16)
                            else:
                                right[n * GROUP : (n + 2) * GROUP, at] = jnp.concatenate(both, axis=0).astype(BF16)
                        now, last = tuple(twice * a - z for a, z in zip(after, now)), after
                if chunk > 0 and (i + 1) % ((chans * 2 // len(bufs)) // PARTS) == 0:
                    multiply(chunk - 1, i // ((chans * 2 // len(bufs)) // PARTS), PARTS)
        for part in range(PARTS):
            multiply(len(bufs) // 2 - 1, part, PARTS)
        own = jnp.where(same, acc[...], 0.0).astype(BF16)
        wide = jnp.dot(own[: SUB * GROUP], place[0], preferred_element_type=F32)
        wide += jnp.dot(own[SUB * GROUP :], place[1], preferred_element_type=F32)
        skies = jnp.dot(gather, wide.astype(BF16), preferred_element_type=F32).astype(BF16)
        for p in range(GROUP // CAP):
            out_ref[GROUP // CAP * group + p, :SUB, :] = skies[p * SUB : (p + 1) * SUB]
            out_ref[GROUP // CAP * group + p, SUB:, :] = ids[p].astype(BF16)


def form_skies(vis, coords, block_fill, block_sub, freq, tiles):
    blocks, parts, lanes = vis.shape
    chans = parts // 2
    chunks = 8
    hbm = pl.BlockSpec(memory_space=pltpu.HBM)
    vmem = pl.BlockSpec(memory_space=pltpu.VMEM)
    bufs = []
    for _ in range(chunks):
        bufs.append(pltpu.VMEM((2 * SUB * GROUP, chans // chunks * lanes), BF16))
        bufs.append(pltpu.VMEM((SUB * GROUP, chans // chunks * lanes), BF16))
    return pl.pallas_call(
        functools.partial(sky_kernel, tiles),
        in_specs=[hbm] * 5,
        out_specs=vmem,
        scratch_shapes=[
            pltpu.SMEM(block_sub.shape, jnp.int32),
            pltpu.SMEM(block_fill.shape, jnp.int32),
            pltpu.SMEM(freq.shape, F32),
            pltpu.VMEM(vis.shape, BF16),
            pltpu.VMEM(coords.shape, BF16),
            pltpu.SMEM((CAP * tiles,), jnp.int32),
            pltpu.SMEM((tiles,), jnp.int32),
            pltpu.SemaphoreType.DMA((5,)),
            pltpu.VMEM((GROUP * (parts + 1) + 7, lanes), F32),
            pltpu.VMEM((2, GROUP, lanes), F32),
            pltpu.VMEM((2 * SUB * GROUP, SUB * GROUP), F32),
        ] + bufs,
        out_shape=jax.ShapeDtypeStruct((tiles, ROWS, 4 * SUB), BF16),
        compiler_params=pltpu.CompilerParams(vmem_limit_bytes=LIMIT),
        name="skies",
    )(block_sub, block_fill, freq, vis, coords)


def fold_matrix():
    shape = (8 * SUB, 4 * SUB)
    row, lane = lax.broadcasted_iota(jnp.int32, shape, 0), lax.broadcasted_iota(jnp.int32, shape, 1)
    h, p = row % HALF, lane % SUB
    taper = (2 * h + 1).astype(F32) / SUB
    taper = 2.0 - 1.8 * taper * taper
    turns = ((p * (2 * h + 1) + 32) & 63) - 32
    cosine, sine = cis(turns.astype(F32) / 64)
    fits = (row // (4 * SUB) == lane // SUB % 2) & (row // SUB % 2 == lane // (2 * SUB))
    return jnp.where(fits, taper * jnp.where(row % SUB < HALF, cosine, sine), 0.0)


def sum_kernel(got_ref, phase_ref, out_ref, acc):
    tiles = got_ref.shape[0]
    acc[...] = jnp.zeros_like(acc)
    for sender in range(tiles):
        data = got_ref[sender, :SUB, :].astype(F32)
        ids = got_ref[sender, SUB:, :].astype(F32)[:1]
        for sub in range(SPP):
            at = slice(sub // 2 * SUB, (sub // 2 + 1) * SUB)
            lanes = slice(sub % 2 * 4 * SUB, (sub % 2 + 1) * 4 * SUB)
            acc[at, lanes] += jnp.where(ids == sub, data, 0.0)
    made = lax.dot_general(
        acc[...], fold_matrix(), (((1,), (0,)), ((), ())),
        precision=lax.Precision.HIGHEST, preferred_element_type=F32,
    )
    turned = pltpu.roll(made, 2 * SUB, 1)
    for pair in range(SPP // 2):
        at = slice(pair * SUB, (pair + 1) * SUB)
        other = SPP // 2 + pair
        out_ref[at, :] = (made[at] * phase_ref[pair : pair + 1] + turned[at] * phase_ref[other : other + 1]).astype(BF16)


def sum_subgrids(got, phase):
    vmem = pl.BlockSpec(memory_space=pltpu.VMEM)
    return pl.pallas_call(
        sum_kernel,
        in_specs=[vmem] * 2,
        out_specs=vmem,
        out_shape=jax.ShapeDtypeStruct((SPP // 2 * SUB, 4 * SUB), BF16),
        scratch_shapes=[pltpu.VMEM((SPP // 2 * SUB, 8 * SUB), F32)],
        compiler_params=pltpu.CompilerParams(vmem_limit_bytes=SMALL),
        name="sums",
    )(got, phase)


def column_phases(norm, tiles, ctrl_ref, w_ref, phase_ref):
    subs = SPP * tiles
    lane = lax.broadcasted_iota(jnp.int32, (SPP, 4 * SUB), 1)
    row = lax.broadcasted_iota(jnp.int32, (SPP, 4 * SUB), 0)
    column = lane % SUB
    odd = lane // SUB % 2
    first = jnp.zeros((SPP, 4 * SUB), jnp.int32)
    w = jnp.zeros((SPP, 4 * SUB), F32)
    for sub in range(SPP):
        here = (row % (SPP // 2) == sub // 2) & (odd == sub % 2)
        s = sub * tiles + ctrl_ref[3 * subs]
        first = jnp.where(here, ctrl_ref[subs + s], first)
        w = jnp.where(here, w_ref[0, ctrl_ref[2 * subs + s]], w)
    x = (first + column).astype(F32) / NCOL - 0.5
    turns = w * (x * x) - ((31 * column) & 63).astype(F32) / 64
    c_re, c_im = cis(turns - jnp.round(turns))
    c_im = jnp.where(lane < 2 * SUB, -c_im, c_im)
    phase_ref[...] = jnp.where(row < SPP // 2, c_re, c_im) * norm


def phase_kernel(norm, tiles, ctrl_ref, w_ref, mat_ref, turn_ref, base_ref, phase_ref):
    subs, rows = turn_ref.shape[1:]
    column_phases(norm, tiles, ctrl_ref, w_ref, phase_ref)
    first = ctrl_ref[3 * subs] * rows
    for k in range(subs):
        s = k % SPP * tiles + k // SPP
        turn_ref[0, k : k + 1, :] = jnp.full((1, rows), ctrl_ref[s].astype(F32))
        turn_ref[1, k : k + 1, :] = jnp.full((1, rows), w_ref[0, ctrl_ref[2 * subs + s]])
    gy = turn_ref[0].astype(jnp.int32)
    q = first + lax.broadcasted_iota(jnp.int32, (subs, rows), 1)
    steps = (q * gy + NV // 2) & (NV - 1)
    pos = q.astype(F32) / NV - 0.5
    turns = (NV // 2 - steps).astype(F32) / NV + turn_ref[1] * (pos * pos)
    turn_ref[0], turn_ref[1] = cis(turns - jnp.round(turns))
    q = first + lax.broadcasted_iota(jnp.int32, (SUB, rows), 1)
    r = lax.broadcasted_iota(jnp.int32, (SUB, rows), 0)
    steps = ((q + 31 * NV // 64) * r + NV // 2) & (NV - 1)
    for part, value in enumerate(cis((NV // 2 - steps).astype(F32) / NV)):
        base_ref[part] = lax.dot_general(
            mat_ref[...], value, (((1,), (0,)), ((), ())),
            precision=lax.Precision.HIGHEST, preferred_element_type=F32,
        )


def make_phases(ctrl, w_band, norm, tiles):
    rows = NV // tiles
    subs = SPP * tiles
    smem = pl.BlockSpec(memory_space=pltpu.SMEM)
    vmem = pl.BlockSpec(memory_space=pltpu.VMEM)
    return pl.pallas_call(
        functools.partial(phase_kernel, norm, tiles),
        in_specs=[smem] * 2 + [vmem],
        out_specs=[vmem] * 3,
        out_shape=[
            jax.ShapeDtypeStruct((2, subs, rows), F32),
            jax.ShapeDtypeStruct((2, SUB, rows), F32),
            jax.ShapeDtypeStruct((SPP, 4 * SUB), F32),
        ],
        compiler_params=pltpu.CompilerParams(vmem_limit_bytes=LIMIT),
        name="phases",
    )(ctrl, w_band, jnp.asarray(column_matrix().T, F32))


def image_kernel(tiles, sides, first_part, last_part, ctrl_ref, turn_ref, base_ref, *refs):
    zs, refs = refs[: len(sides)], refs[len(sides) :]
    start = None
    if not first_part:
        start, refs = refs[0], refs[1:]
    out_ref, refs = refs[0], refs[1:]
    acc = out_ref
    if last_part:
        acc, refs = refs[0], refs[1:]
    canvas, table = refs
    rows = turn_ref.shape[2]
    subs = SPP * tiles
    me = ctrl_ref[3 * subs]
    depth = tiles // 4
    lane = lax.broadcasted_iota(jnp.int32, (SUB, 4 * SUB), 1)
    base_re, base_im = base_ref[0], base_ref[1]
    acc[...] = jnp.zeros(acc.shape, F32) if first_part else start[...]
    for side, z_ref in zip(sides, zs):

        @pl.loop(0, depth, unroll=4)
        def _(t):
            panel = ((me // 4 - t) & (depth - 1)) * 4 + ((me & 3) ^ side)
            for pair in range(SPP // 2):
                z = z_ref[t, pair * SUB : (pair + 1) * SUB, :].astype(F32)
                for odd in range(2):
                    sub = 2 * pair + odd
                    first = ctrl_ref[subs + sub * tiles + panel]
                    moved = pltpu.roll(z, (first - odd * SUB + 4 * SUB) & (4 * SUB - 1), 1)
                    place = (lane & (NCOL - 1)) - first
                    canvas[sub * SUB : (sub + 1) * SUB, :] = jnp.where((place >= 0) & (place < SUB), moved, 0.0)
            turn_re = turn_ref[0, pl.ds(panel * SPP, SPP), :]
            turn_im = turn_ref[1, pl.ds(panel * SPP, SPP), :]
            for sub in range(SPP):
                at = slice(sub * SUB, (sub + 1) * SUB)
                t_re, t_im = turn_re[sub : sub + 1], turn_im[sub : sub + 1]
                table[at, :rows] = (t_re * base_re - t_im * base_im).astype(BF16)
                table[at, rows:] = (t_re * base_im + t_im * base_re).astype(BF16)
            acc[...] += jnp.dot(canvas[...].T.astype(BF16), table[...], preferred_element_type=F32)

    if last_part:
        real = acc[:NCOL, :rows] - acc[NCOL:, rows:]
        imag = acc[NCOL:, :rows] + acc[:NCOL, rows:]
        out_ref[...] = jnp.concatenate([real, imag], axis=0).T


def make_image(ctrl, turn, base, zs, sides, tiles, start=None, last=False):
    rows = turn.shape[2]
    smem = pl.BlockSpec(memory_space=pltpu.SMEM)
    vmem = pl.BlockSpec(memory_space=pltpu.VMEM)
    carry = [] if start is None else [start]
    scratch = [
        pltpu.VMEM((4 * SUB, 2 * rows), F32),
        pltpu.VMEM((SPP * SUB, 4 * SUB), F32),
        pltpu.VMEM((SPP * SUB, 2 * rows), BF16),
    ]
    return pl.pallas_call(
        functools.partial(image_kernel, tiles, sides, start is None, last),
        in_specs=[smem] + [vmem] * (2 + len(zs) + len(carry)),
        out_specs=vmem,
        out_shape=jax.ShapeDtypeStruct((rows, 4 * SUB) if last else (4 * SUB, 2 * rows), F32),
        scratch_shapes=scratch if last else scratch[1:],
        compiler_params=pltpu.CompilerParams(vmem_limit_bytes=SMALL),
        name="image",
    )(ctrl, turn, base, *zs, *carry)


def shards(vis, coords, block_fill, block_sub, sub_pos, sub_plane, freq, plane_w):
    tiles = lax.axis_size("tile")
    me = lax.axis_index("tile").reshape(1)
    norm = 1.0 / (math.sqrt(vis.shape[2] // 2 * vis.shape[3]) * SUB * math.sqrt(NV))
    skies = form_skies(vis[0], coords, block_fill, block_sub, freq, tiles)
    ctrl = jnp.concatenate([sub_pos[:, 0], sub_pos[:, 1], sub_plane, me])
    turn, base, phase = make_phases(ctrl, plane_w, norm, tiles)
    got = lax.all_to_all(skies, "tile", split_axis=0, concat_axis=0, tiled=True)
    z = sum_subgrids(got, phase)
    depth = tiles // 4
    ahead = lambda i, t: (i // 4 + t) % depth * 4 + i % 4
    column = [z] + [lax.ppermute(z, "tile", [(i, ahead(i, t)) for i in range(tiles)]) for t in range(1, depth)]
    column = jnp.stack(column)
    beside = [(i, i ^ 1) for i in range(tiles)]
    across = lax.ppermute(column, "tile", [(i, i ^ 2) for i in range(tiles)])
    twin = lax.ppermute(column, "tile", beside)
    part = make_image(ctrl, turn, base, [column, twin], [0, 1], tiles)
    across, part = lax.optimization_barrier((across, part))
    far = lax.ppermute(across, "tile", beside)
    part = make_image(ctrl, turn, base, [across], [2], tiles, part)
    return make_image(ctrl, turn, base, [far], [3], tiles, part, True)[None]


def solution(mesh):
    return jax.shard_map(
        shards,
        mesh=mesh,
        in_specs=(
            P("band", "tile", None, None),
            P("tile", None, None),
            P("tile"),
            P("tile"),
            P(),
            P(),
            P("band", None),
            P("band", None),
        ),
        out_specs=P("band", "tile", None),
        check_vma=False,
    )
```

```python
import functools
import math

import jax
import jax.numpy as jnp
import numpy as np
from jax import lax
from jax.experimental import pallas as pl
from jax.experimental.pallas import tpu as pltpu
from jax.sharding import PartitionSpec as P

SUB = 32
HALF = SUB // 2
CAP = 2
NV = 8192
NCOL = 64
SPP = 8
ROWS = 40
GROUP = 8
LIMIT = 60 * 2**20
SMALL = 16 * 2**20
F32 = jnp.float32
BF16 = jnp.bfloat16


def poly(x2, coefs):
    acc = jnp.full_like(x2, coefs[-1])
    for coef in coefs[-2::-1]:
        acc = acc * x2 + coef
    return acc


def sincos(x, terms):
    x2 = x * x
    sine = x * poly(x2, [(-1.0) ** k / math.factorial(2 * k + 1) for k in range(terms)])
    cosine = poly(x2, [(-1.0) ** k / math.factorial(2 * k) for k in range(terms + 1)])
    return sine, cosine


def small_sincos(x):
    x2 = x * x
    sine = x * poly(x2, [1.0, -0.1666663012624129, 0.00833098262499725, -0.00019386139634034114])
    cosine = poly(x2, [1.0, -0.49999999215877833, 0.041666570358134106, -0.0013885254406105342, 2.426341201481312e-05])
    return sine, cosine


def cis(turns):
    sine, cosine = sincos(turns * math.pi, 6)
    return 1.0 - 2.0 * sine * sine, 2.0 * sine * cosine


def column_matrix():
    p = np.arange(SUB)[:, None]
    h = np.arange(HALF)[None, :]
    taper = 1.0 - 0.9 * ((2 * h + 1) / SUB) ** 2
    angle = 2.0 * np.pi * p * (h + 0.5) / SUB
    return np.concatenate([2 * taper * np.cos(angle), 2 * taper * np.sin(angle)], axis=1)


def pick_matrices():
    iota = lambda shape, dim: lax.broadcasted_iota(jnp.int32, shape, dim)
    one = lambda mask: jnp.where(mask, 1.0, 0.0).astype(BF16)
    shape = (SUB * GROUP, 4 * SUB)
    k, lane = iota(shape, 0), iota(shape, 1)
    fits = (k // GROUP == lane % SUB) & (k % CAP == lane // (2 * SUB))
    place = [one(fits & (lane // SUB % 2 == part)) for part in range(2)]
    shape = (GROUP // CAP * SUB, SUB * GROUP)
    r, k = iota(shape, 0), iota(shape, 1)
    return place, one((r % SUB == k // GROUP) & (r // SUB == k % GROUP // CAP))


def sky_kernel(tiles, sub_hbm, fill_hbm, freq_hbm, vis_hbm, coord_hbm, out_ref,
               sub_ref, fill_ref, freq_ref, vis_ref, coord_ref, blk, count, sems, volt, uv, acc, own_ref, *bufs):
    blocks = vis_ref.shape[0]
    chans = vis_ref.shape[1] // 2
    lanes = vis_ref.shape[2]
    step = 2 * chans + 1
    pairs = ((sub_hbm, sub_ref), (fill_hbm, fill_ref), (freq_hbm, freq_ref), (coord_hbm, coord_ref), (vis_hbm, vis_ref))
    copies = [pltpu.make_async_copy(a, b, sems.at[i]) for i, (a, b) in enumerate(pairs)]
    for copy in copies:
        copy.start()

    @pl.loop(0, tiles)
    def _(i):
        count[i] = 0
        for j in range(CAP):
            blk[CAP * i + j] = -1

    for copy in copies[:2]:
        copy.wait()

    @pl.loop(0, blocks)
    def _(b):
        p = sub_ref[b] & (tiles - 1)
        have = count[p]
        blk[CAP * p + have] = b
        count[p] = have + 1

    for copy in copies[2:]:
        copy.wait()

    place, gather = pick_matrices()
    lane = lax.broadcasted_iota(jnp.int32, (GROUP, lanes), 1)
    row = lax.broadcasted_iota(jnp.int32, (GROUP, lanes), 0)
    lane16 = lax.broadcasted_iota(jnp.int32, (ROWS - SUB, 4 * SUB), 1)
    same = (lax.broadcasted_iota(jnp.int32, (2 * SUB * GROUP, SUB * GROUP), 0) % GROUP
            == lax.broadcasted_iota(jnp.int32, (2 * SUB * GROUP, SUB * GROUP), 1) % GROUP)

    def finish(group):
        wide = jnp.dot(own_ref[: SUB * GROUP], place[0], preferred_element_type=F32)
        wide += jnp.dot(own_ref[SUB * GROUP :], place[1], preferred_element_type=F32)
        skies = jnp.dot(gather, wide.astype(BF16), preferred_element_type=F32).astype(BF16)
        for p in range(GROUP // CAP):
            out_ref[GROUP // CAP * group + p, :SUB, :] = skies[p * SUB : (p + 1) * SUB]

    own_ref[...] = jnp.zeros_like(own_ref)

    @pl.loop(0, CAP * tiles // GROUP)
    def _(group):
        live = jnp.zeros((GROUP, lanes), jnp.int32)
        ids = [jnp.zeros((ROWS - SUB, 4 * SUB), F32) for _ in range(GROUP // CAP)]
        for s in range(GROUP):
            which = blk[GROUP * group + s]
            b = jnp.maximum(which, 0)
            live = jnp.where(row == s, jnp.where(which < 0, 0, fill_ref[b]), live)
            local = (sub_ref[b] >> (tiles.bit_length() - 1)).astype(F32)
            ids[s // CAP] = jnp.where(lane16 // (2 * SUB) == s % CAP, local, ids[s // CAP])
            coord = coord_ref[b].astype(F32)
            uv[0, s : s + 1, :] = coord[:1]
            uv[1, s : s + 1, :] = coord[1:]
            volt[s * step : s * step + 2 * chans, :] = vis_ref[b].astype(F32)
        for p in range(GROUP // CAP):
            out_ref[GROUP // CAP * group + p, SUB:, :] = ids[p].astype(BF16)
        keep = lane < live
        finish(jnp.maximum(group - 1, 0))
        steps = [uv[axis] * (math.pi / SUB) for axis in range(2)]
        def multiply(chunk, part, parts):
            at = slice(part * 2 * SUB * GROUP // parts, (part + 1) * 2 * SUB * GROUP // parts)
            made = lax.dot_general(
                bufs[2 * chunk][at, :], bufs[2 * chunk + 1][...], (((1,), (1,)), ((), ())), preferred_element_type=F32
            )
            if chunk == 0:
                acc[at, :] = made
            else:
                acc[at, :] += made

        PARTS = 2
        for chunk in range(len(bufs) // 2):
            left, right = bufs[2 * chunk : 2 * chunk + 2]
            for i in range(chans * 2 // len(bufs)):
                c = chunk * (chans * 2 // len(bufs)) + i
                at = slice(i * lanes, (i + 1) * lanes)
                (su, cu), (sv, cv) = [small_sincos(value * freq_ref[0, c]) for value in steps]
                turn_re = cu * cv - su * sv
                turn_im = su * cv + cu * sv
                w_re = jnp.where(keep, volt[pl.ds(c, GROUP, stride=step), :], 0.0)
                w_im = jnp.where(keep, volt[pl.ds(chans + c, GROUP, stride=step), :], 0.0)
                w = (w_re * turn_re + w_im * turn_im, w_im * turn_re - w_re * turn_im)
                for axis, (sine, cosine) in enumerate(((su, cu), (sv, cv))):
                    twice = 2.0 - 4.0 * sine * sine
                    now = (cosine, sine)
                    last = (cosine, -sine)
                    for h in range(0, HALF, 2):
                        after = tuple(twice * a - z for a, z in zip(now, last))
                        for trig in range(2):
                            both = (now[trig], after[trig])
                            n = trig * HALF + h
                            if axis == 0:
                                for part in range(2):
                                    r = (part * SUB + n) * GROUP
                                    left[r : r + 2 * GROUP, at] = jnp.concatenate(
                                        [w[part] * x for x in both], axis=0
                                    ).astype(BF16)
                            else:
                                right[n * GROUP : (n + 2) * GROUP, at] = jnp.concatenate(both, axis=0).astype(BF16)
                        now, last = tuple(twice * a - z for a, z in zip(after, now)), after
                if chunk > 0 and (i + 1) % ((chans * 2 // len(bufs)) // PARTS) == 0:
                    multiply(chunk - 1, i // ((chans * 2 // len(bufs)) // PARTS), PARTS)
        for part in range(PARTS):
            multiply(len(bufs) // 2 - 1, part, PARTS)
        own_ref[...] = jnp.where(same, acc[...], 0.0).astype(BF16)

    finish(out_ref.shape[0] * 2 // GROUP - 1)


def form_skies(vis, coords, block_fill, block_sub, freq, tiles):
    blocks, parts, lanes = vis.shape
    chans = parts // 2
    chunks = 8
    hbm = pl.BlockSpec(memory_space=pltpu.HBM)
    vmem = pl.BlockSpec(memory_space=pltpu.VMEM)
    bufs = []
    for _ in range(chunks):
        bufs.append(pltpu.VMEM((2 * SUB * GROUP, chans // chunks * lanes), BF16))
        bufs.append(pltpu.VMEM((SUB * GROUP, chans // chunks * lanes), BF16))
    return pl.pallas_call(
        functools.partial(sky_kernel, tiles),
        in_specs=[hbm] * 5,
        out_specs=vmem,
        scratch_shapes=[
            pltpu.SMEM(block_sub.shape, jnp.int32),
            pltpu.SMEM(block_fill.shape, jnp.int32),
            pltpu.SMEM(freq.shape, F32),
            pltpu.VMEM(vis.shape, BF16),
            pltpu.VMEM(coords.shape, BF16),
            pltpu.SMEM((CAP * tiles,), jnp.int32),
            pltpu.SMEM((tiles,), jnp.int32),
            pltpu.SemaphoreType.DMA((5,)),
            pltpu.VMEM((GROUP * (parts + 1) + 7, lanes), F32),
            pltpu.VMEM((2, GROUP, lanes), F32),
            pltpu.VMEM((2 * SUB * GROUP, SUB * GROUP), F32),
            pltpu.VMEM((2 * SUB * GROUP, SUB * GROUP), BF16),
        ] + bufs,
        out_shape=jax.ShapeDtypeStruct((tiles, ROWS, 4 * SUB), BF16),
        compiler_params=pltpu.CompilerParams(vmem_limit_bytes=LIMIT),
        name="skies",
    )(block_sub, block_fill, freq, vis, coords)


def fold_matrix():
    shape = (8 * SUB, 4 * SUB)
    row, lane = lax.broadcasted_iota(jnp.int32, shape, 0), lax.broadcasted_iota(jnp.int32, shape, 1)
    h, p = row % HALF, lane % SUB
    taper = (2 * h + 1).astype(F32) / SUB
    taper = 2.0 - 1.8 * taper * taper
    turns = ((p * (2 * h + 1) + 32) & 63) - 32
    cosine, sine = cis(turns.astype(F32) / 64)
    fits = (row // (4 * SUB) == lane // SUB % 2) & (row // SUB % 2 == lane // (2 * SUB))
    return jnp.where(fits, taper * jnp.where(row % SUB < HALF, cosine, sine), 0.0)


def sum_kernel(got_ref, phase_ref, out_ref, acc):
    tiles = got_ref.shape[0]
    acc[...] = jnp.zeros_like(acc)
    for sender in range(tiles):
        data = got_ref[sender, :SUB, :].astype(F32)
        ids = got_ref[sender, SUB:, :].astype(F32)[:1]
        for sub in range(SPP):
            at = slice(sub // 2 * SUB, (sub // 2 + 1) * SUB)
            lanes = slice(sub % 2 * 4 * SUB, (sub % 2 + 1) * 4 * SUB)
            acc[at, lanes] += jnp.where(ids == sub, data, 0.0)
    made = lax.dot_general(
        acc[...], fold_matrix(), (((1,), (0,)), ((), ())),
        precision=lax.Precision.HIGHEST, preferred_element_type=F32,
    )
    turned = pltpu.roll(made, 2 * SUB, 1)
    for pair in range(SPP // 2):
        at = slice(pair * SUB, (pair + 1) * SUB)
        other = SPP // 2 + pair
        out_ref[at, :] = (made[at] * phase_ref[pair : pair + 1] + turned[at] * phase_ref[other : other + 1]).astype(BF16)


def sum_subgrids(got, phase):
    vmem = pl.BlockSpec(memory_space=pltpu.VMEM)
    return pl.pallas_call(
        sum_kernel,
        in_specs=[vmem] * 2,
        out_specs=vmem,
        out_shape=jax.ShapeDtypeStruct((SPP // 2 * SUB, 4 * SUB), BF16),
        scratch_shapes=[pltpu.VMEM((SPP // 2 * SUB, 8 * SUB), F32)],
        compiler_params=pltpu.CompilerParams(vmem_limit_bytes=SMALL),
        name="sums",
    )(got, phase)


def column_phases(norm, tiles, ctrl_ref, w_ref, phase_ref):
    subs = SPP * tiles
    lane = lax.broadcasted_iota(jnp.int32, (SPP, 4 * SUB), 1)
    row = lax.broadcasted_iota(jnp.int32, (SPP, 4 * SUB), 0)
    column = lane % SUB
    odd = lane // SUB % 2
    first = jnp.zeros((SPP, 4 * SUB), jnp.int32)
    w = jnp.zeros((SPP, 4 * SUB), F32)
    for sub in range(SPP):
        here = (row % (SPP // 2) == sub // 2) & (odd == sub % 2)
        s = sub * tiles + ctrl_ref[3 * subs]
        first = jnp.where(here, ctrl_ref[subs + s], first)
        w = jnp.where(here, w_ref[0, ctrl_ref[2 * subs + s]], w)
    x = (first + column).astype(F32) / NCOL - 0.5
    turns = w * (x * x) - ((31 * column) & 63).astype(F32) / 64
    c_re, c_im = cis(turns - jnp.round(turns))
    c_im = jnp.where(lane < 2 * SUB, -c_im, c_im)
    phase_ref[...] = jnp.where(row < SPP // 2, c_re, c_im) * norm


def phase_kernel(norm, tiles, ctrl_ref, w_ref, mat_ref, turn_ref, base_ref, phase_ref):
    subs, rows = turn_ref.shape[1:]
    column_phases(norm, tiles, ctrl_ref, w_ref, phase_ref)
    first = ctrl_ref[3 * subs] * rows
    for k in range(subs):
        s = k % SPP * tiles + k // SPP
        turn_ref[0, k : k + 1, :] = jnp.full((1, rows), ctrl_ref[s].astype(F32))
        turn_ref[1, k : k + 1, :] = jnp.full((1, rows), w_ref[0, ctrl_ref[2 * subs + s]])
    gy = turn_ref[0].astype(jnp.int32)
    q = first + lax.broadcasted_iota(jnp.int32, (subs, rows), 1)
    steps = (q * gy + NV // 2) & (NV - 1)
    pos = q.astype(F32) / NV - 0.5
    turns = (NV // 2 - steps).astype(F32) / NV + turn_ref[1] * (pos * pos)
    turn_ref[0], turn_ref[1] = cis(turns - jnp.round(turns))
    q = first + lax.broadcasted_iota(jnp.int32, (SUB, rows), 1)
    r = lax.broadcasted_iota(jnp.int32, (SUB, rows), 0)
    steps = ((q + 31 * NV // 64) * r + NV // 2) & (NV - 1)
    for part, value in enumerate(cis((NV // 2 - steps).astype(F32) / NV)):
        base_ref[part] = lax.dot_general(
            mat_ref[...], value, (((1,), (0,)), ((), ())),
            precision=lax.Precision.HIGHEST, preferred_element_type=F32,
        )


def make_phases(ctrl, w_band, norm, tiles):
    rows = NV // tiles
    subs = SPP * tiles
    smem = pl.BlockSpec(memory_space=pltpu.SMEM)
    vmem = pl.BlockSpec(memory_space=pltpu.VMEM)
    return pl.pallas_call(
        functools.partial(phase_kernel, norm, tiles),
        in_specs=[smem] * 2 + [vmem],
        out_specs=[vmem] * 3,
        out_shape=[
            jax.ShapeDtypeStruct((2, subs, rows), F32),
            jax.ShapeDtypeStruct((2, SUB, rows), F32),
            jax.ShapeDtypeStruct((SPP, 4 * SUB), F32),
        ],
        compiler_params=pltpu.CompilerParams(vmem_limit_bytes=LIMIT),
        name="phases",
    )(ctrl, w_band, jnp.asarray(column_matrix().T, F32))


def image_kernel(tiles, sides, first_part, last_part, ctrl_ref, turn_ref, base_ref, *refs):
    zs, refs = refs[: len(sides)], refs[len(sides) :]
    start = None
    if not first_part:
        start, refs = refs[0], refs[1:]
    out_ref, refs = refs[0], refs[1:]
    acc = out_ref
    if last_part:
        acc, refs = refs[0], refs[1:]
    canvas, table = refs
    rows = turn_ref.shape[2]
    subs = SPP * tiles
    me = ctrl_ref[3 * subs]
    depth = tiles // 4
    lane = lax.broadcasted_iota(jnp.int32, (SUB, 4 * SUB), 1)
    base_re, base_im = base_ref[0], base_ref[1]
    acc[...] = jnp.zeros(acc.shape, F32) if first_part else start[...]
    for side, z_ref in zip(sides, zs):

        @pl.loop(0, depth, unroll=4)
        def _(t):
            panel = ((me // 4 - t) & (depth - 1)) * 4 + ((me & 3) ^ side)
            for pair in range(SPP // 2):
                z = z_ref[t, pair * SUB : (pair + 1) * SUB, :].astype(F32)
                for odd in range(2):
                    sub = 2 * pair + odd
                    first = ctrl_ref[subs + sub * tiles + panel]
                    moved = pltpu.roll(z, (first - odd * SUB + 4 * SUB) & (4 * SUB - 1), 1)
                    place = (lane & (NCOL - 1)) - first
                    canvas[sub * SUB : (sub + 1) * SUB, :] = jnp.where((place >= 0) & (place < SUB), moved, 0.0)
            turn_re = turn_ref[0, pl.ds(panel * SPP, SPP), :]
            turn_im = turn_ref[1, pl.ds(panel * SPP, SPP), :]
            for sub in range(SPP):
                at = slice(sub * SUB, (sub + 1) * SUB)
                t_re, t_im = turn_re[sub : sub + 1], turn_im[sub : sub + 1]
                table[at, :rows] = (t_re * base_re - t_im * base_im).astype(BF16)
                table[at, rows:] = (t_re * base_im + t_im * base_re).astype(BF16)
            acc[...] += jnp.dot(canvas[...].T.astype(BF16), table[...], preferred_element_type=F32)

    if last_part:
        real = acc[:NCOL, :rows] - acc[NCOL:, rows:]
        imag = acc[NCOL:, :rows] + acc[:NCOL, rows:]
        out_ref[...] = jnp.concatenate([real, imag], axis=0).T


def make_image(ctrl, turn, base, zs, sides, tiles, start=None, last=False):
    rows = turn.shape[2]
    smem = pl.BlockSpec(memory_space=pltpu.SMEM)
    vmem = pl.BlockSpec(memory_space=pltpu.VMEM)
    carry = [] if start is None else [start]
    scratch = [
        pltpu.VMEM((4 * SUB, 2 * rows), F32),
        pltpu.VMEM((SPP * SUB, 4 * SUB), F32),
        pltpu.VMEM((SPP * SUB, 2 * rows), BF16),
    ]
    return pl.pallas_call(
        functools.partial(image_kernel, tiles, sides, start is None, last),
        in_specs=[smem] + [vmem] * (2 + len(zs) + len(carry)),
        out_specs=vmem,
        out_shape=jax.ShapeDtypeStruct((rows, 4 * SUB) if last else (4 * SUB, 2 * rows), F32),
        scratch_shapes=scratch if last else scratch[1:],
        compiler_params=pltpu.CompilerParams(vmem_limit_bytes=SMALL),
        name="image",
    )(ctrl, turn, base, *zs, *carry)


def shards(vis, coords, block_fill, block_sub, sub_pos, sub_plane, freq, plane_w):
    tiles = lax.axis_size("tile")
    me = lax.axis_index("tile").reshape(1)
    norm = 1.0 / (math.sqrt(vis.shape[2] // 2 * vis.shape[3]) * SUB * math.sqrt(NV))
    skies = form_skies(vis[0], coords, block_fill, block_sub, freq, tiles)
    ctrl = jnp.concatenate([sub_pos[:, 0], sub_pos[:, 1], sub_plane, me])
    turn, base, phase = make_phases(ctrl, plane_w, norm, tiles)
    got = lax.all_to_all(skies, "tile", split_axis=0, concat_axis=0, tiled=True)
    z = sum_subgrids(got, phase)
    depth = tiles // 4
    ahead = lambda i, t: (i // 4 + t) % depth * 4 + i % 4
    column = [z] + [lax.ppermute(z, "tile", [(i, ahead(i, t)) for i in range(tiles)]) for t in range(1, depth)]
    column = jnp.stack(column)
    beside = [(i, i ^ 1) for i in range(tiles)]
    across = lax.ppermute(column, "tile", [(i, i ^ 2) for i in range(tiles)])
    twin = lax.ppermute(column, "tile", beside)
    part = make_image(ctrl, turn, base, [column, twin], [0, 1], tiles)
    across, part = lax.optimization_barrier((across, part))
    far = lax.ppermute(across, "tile", beside)
    part = make_image(ctrl, turn, base, [across], [2], tiles, part)
    return make_image(ctrl, turn, base, [far], [3], tiles, part, True)[None]


def solution(mesh):
    return jax.shard_map(
        shards,
        mesh=mesh,
        in_specs=(
            P("band", "tile", None, None),
            P("tile", None, None),
            P("tile"),
            P("tile"),
            P(),
            P(),
            P("band", None),
            P("band", None),
        ),
        out_specs=P("band", "tile", None),
        check_vma=False,
    )
```

```python
import functools
import math

import jax
import jax.numpy as jnp
import numpy as np
from jax import lax
from jax.experimental import pallas as pl
from jax.experimental.pallas import tpu as pltpu
from jax.sharding import PartitionSpec as P

SUB = 32
HALF = SUB // 2
CAP = 2
NV = 8192
NCOL = 64
SPP = 8
ROWS = 40
GROUP = 8
LIMIT = 60 * 2**20
SMALL = 16 * 2**20
F32 = jnp.float32
BF16 = jnp.bfloat16


def poly(x2, coefs):
    acc = jnp.full_like(x2, coefs[-1])
    for coef in coefs[-2::-1]:
        acc = acc * x2 + coef
    return acc


def sincos(x, terms):
    x2 = x * x
    sine = x * poly(x2, [(-1.0) ** k / math.factorial(2 * k + 1) for k in range(terms)])
    cosine = poly(x2, [(-1.0) ** k / math.factorial(2 * k) for k in range(terms + 1)])
    return sine, cosine


def small_sincos(x):
    x2 = x * x
    sine = x * poly(x2, [1.0, -0.1666663012624129, 0.00833098262499725, -0.00019386139634034114])
    cosine = poly(x2, [1.0, -0.49999999215877833, 0.041666570358134106, -0.0013885254406105342, 2.426341201481312e-05])
    return sine, cosine


def cis(turns):
    sine, cosine = sincos(turns * math.pi, 6)
    return 1.0 - 2.0 * sine * sine, 2.0 * sine * cosine


def column_matrix():
    p = np.arange(SUB)[:, None]
    h = np.arange(HALF)[None, :]
    taper = 1.0 - 0.9 * ((2 * h + 1) / SUB) ** 2
    angle = 2.0 * np.pi * p * (h + 0.5) / SUB
    return np.concatenate([2 * taper * np.cos(angle), 2 * taper * np.sin(angle)], axis=1)


def pick_matrices():
    iota = lambda shape, dim: lax.broadcasted_iota(jnp.int32, shape, dim)
    one = lambda mask: jnp.where(mask, 1.0, 0.0).astype(BF16)
    shape = (SUB * GROUP, 4 * SUB)
    k, lane = iota(shape, 0), iota(shape, 1)
    fits = (k // GROUP == lane % SUB) & (k % CAP == lane // (2 * SUB))
    place = [one(fits & (lane // SUB % 2 == part)) for part in range(2)]
    shape = (GROUP // CAP * SUB, SUB * GROUP)
    r, k = iota(shape, 0), iota(shape, 1)
    return place, one((r % SUB == k // GROUP) & (r // SUB == k % GROUP // CAP))


def sky_kernel(tiles, sub_hbm, fill_hbm, freq_hbm, vis_hbm, coord_hbm, out_ref,
               sub_ref, fill_ref, freq_ref, vis_ref, coord_ref, blk, count, sems, volt, uv, acc, own_ref, *bufs):
    blocks = vis_ref.shape[0]
    chans = vis_ref.shape[1] // 2
    lanes = vis_ref.shape[2]
    step = 2 * chans + 1
    pairs = ((sub_hbm, sub_ref), (fill_hbm, fill_ref), (freq_hbm, freq_ref), (coord_hbm, coord_ref), (vis_hbm, vis_ref))
    copies = [pltpu.make_async_copy(a, b, sems.at[i]) for i, (a, b) in enumerate(pairs)]
    for copy in copies:
        copy.start()

    @pl.loop(0, tiles)
    def _(i):
        count[i] = 0
        for j in range(CAP):
            blk[CAP * i + j] = -1

    for copy in copies[:2]:
        copy.wait()

    @pl.loop(0, blocks)
    def _(b):
        p = sub_ref[b] & (tiles - 1)
        have = count[p]
        blk[CAP * p + have] = b
        count[p] = have + 1

    for copy in copies[2:]:
        copy.wait()

    place, gather = pick_matrices()
    lane64 = lax.broadcasted_iota(jnp.int32, (2 * chans, lanes), 1)
    lane16 = lax.broadcasted_iota(jnp.int32, (ROWS - SUB, 4 * SUB), 1)
    same = (lax.broadcasted_iota(jnp.int32, (2 * SUB * GROUP, SUB * GROUP), 0) % GROUP
            == lax.broadcasted_iota(jnp.int32, (2 * SUB * GROUP, SUB * GROUP), 1) % GROUP)

    def finish(group):
        wide = jnp.dot(own_ref[: SUB * GROUP], place[0], preferred_element_type=F32)
        wide += jnp.dot(own_ref[SUB * GROUP :], place[1], preferred_element_type=F32)
        skies = jnp.dot(gather, wide.astype(BF16), preferred_element_type=F32).astype(BF16)
        for p in range(GROUP // CAP):
            out_ref[GROUP // CAP * group + p, :SUB, :] = skies[p * SUB : (p + 1) * SUB]

    own_ref[...] = jnp.zeros_like(own_ref)

    @pl.loop(0, CAP * tiles // GROUP)
    def _(group):
        ids = [jnp.zeros((ROWS - SUB, 4 * SUB), F32) for _ in range(GROUP // CAP)]
        for s in range(GROUP):
            which = blk[GROUP * group + s]
            b = jnp.maximum(which, 0)
            local = (sub_ref[b] >> (tiles.bit_length() - 1)).astype(F32)
            ids[s // CAP] = jnp.where(lane16 // (2 * SUB) == s % CAP, local, ids[s // CAP])
            coord = coord_ref[b].astype(F32)
            uv[0, s : s + 1, :] = coord[:1]
            uv[1, s : s + 1, :] = coord[1:]
            rows_live = jnp.where(which < 0, 0, fill_ref[b])
            volt[s * step : s * step + 2 * chans, :] = jnp.where(lane64 < rows_live, vis_ref[b].astype(F32), 0.0)
        for p in range(GROUP // CAP):
            out_ref[GROUP // CAP * group + p, SUB:, :] = ids[p].astype(BF16)
        finish(jnp.maximum(group - 1, 0))
        steps = [uv[axis] * (math.pi / SUB) for axis in range(2)]
        def multiply(chunk, part, parts):
            at = slice(part * 2 * SUB * GROUP // parts, (part + 1) * 2 * SUB * GROUP // parts)
            made = lax.dot_general(
                bufs[2 * chunk][at, :], bufs[2 * chunk + 1][...], (((1,), (1,)), ((), ())), preferred_element_type=F32
            )
            if chunk == 0:
                acc[at, :] = made
            else:
                acc[at, :] += made

        PARTS = 2
        for chunk in range(len(bufs) // 2):
            left, right = bufs[2 * chunk : 2 * chunk + 2]
            for i in range(chans * 2 // len(bufs)):
                c = chunk * (chans * 2 // len(bufs)) + i
                at = slice(i * lanes, (i + 1) * lanes)
                (su, cu), (sv, cv) = [small_sincos(value * freq_ref[0, c]) for value in steps]
                turn_re = cu * cv - su * sv
                turn_im = su * cv + cu * sv
                w_re = volt[pl.ds(c, GROUP, stride=step), :]
                w_im = volt[pl.ds(chans + c, GROUP, stride=step), :]
                w = (w_re * turn_re + w_im * turn_im, w_im * turn_re - w_re * turn_im)
                for axis, (sine, cosine) in enumerate(((su, cu), (sv, cv))):
                    twice = 2.0 - 4.0 * sine * sine
                    now = (cosine, sine)
                    last = (cosine, -sine)
                    for h in range(0, HALF, 2):
                        after = tuple(twice * a - z for a, z in zip(now, last))
                        for trig in range(2):
                            both = (now[trig], after[trig])
                            n = trig * HALF + h
                            if axis == 0:
                                for part in range(2):
                                    r = (part * SUB + n) * GROUP
                                    left[r : r + 2 * GROUP, at] = jnp.concatenate(
                                        [w[part] * x for x in both], axis=0
                                    ).astype(BF16)
                            else:
                                right[n * GROUP : (n + 2) * GROUP, at] = jnp.concatenate(both, axis=0).astype(BF16)
                        now, last = tuple(twice * a - z for a, z in zip(after, now)), after
                if chunk > 0 and (i + 1) % ((chans * 2 // len(bufs)) // PARTS) == 0:
                    multiply(chunk - 1, i // ((chans * 2 // len(bufs)) // PARTS), PARTS)
        for part in range(PARTS):
            multiply(len(bufs) // 2 - 1, part, PARTS)
        own_ref[...] = jnp.where(same, acc[...], 0.0).astype(BF16)

    finish(out_ref.shape[0] * 2 // GROUP - 1)


def form_skies(vis, coords, block_fill, block_sub, freq, tiles):
    blocks, parts, lanes = vis.shape
    chans = parts // 2
    chunks = 8
    hbm = pl.BlockSpec(memory_space=pltpu.HBM)
    vmem = pl.BlockSpec(memory_space=pltpu.VMEM)
    bufs = []
    for _ in range(chunks):
        bufs.append(pltpu.VMEM((2 * SUB * GROUP, chans // chunks * lanes), BF16))
        bufs.append(pltpu.VMEM((SUB * GROUP, chans // chunks * lanes), BF16))
    return pl.pallas_call(
        functools.partial(sky_kernel, tiles),
        in_specs=[hbm] * 5,
        out_specs=vmem,
        scratch_shapes=[
            pltpu.SMEM(block_sub.shape, jnp.int32),
            pltpu.SMEM(block_fill.shape, jnp.int32),
            pltpu.SMEM(freq.shape, F32),
            pltpu.VMEM(vis.shape, BF16),
            pltpu.VMEM(coords.shape, BF16),
            pltpu.SMEM((CAP * tiles,), jnp.int32),
            pltpu.SMEM((tiles,), jnp.int32),
            pltpu.SemaphoreType.DMA((5,)),
            pltpu.VMEM((GROUP * (parts + 1) + 7, lanes), F32),
            pltpu.VMEM((2, GROUP, lanes), F32),
            pltpu.VMEM((2 * SUB * GROUP, SUB * GROUP), F32),
            pltpu.VMEM((2 * SUB * GROUP, SUB * GROUP), BF16),
        ] + bufs,
        out_shape=jax.ShapeDtypeStruct((tiles, ROWS, 4 * SUB), BF16),
        compiler_params=pltpu.CompilerParams(vmem_limit_bytes=LIMIT),
        name="skies",
    )(block_sub, block_fill, freq, vis, coords)


def fold_matrix():
    shape = (8 * SUB, 4 * SUB)
    row, lane = lax.broadcasted_iota(jnp.int32, shape, 0), lax.broadcasted_iota(jnp.int32, shape, 1)
    h, p = row % HALF, lane % SUB
    taper = (2 * h + 1).astype(F32) / SUB
    taper = 2.0 - 1.8 * taper * taper
    turns = ((p * (2 * h + 1) + 32) & 63) - 32
    cosine, sine = cis(turns.astype(F32) / 64)
    fits = (row // (4 * SUB) == lane // SUB % 2) & (row // SUB % 2 == lane // (2 * SUB))
    return jnp.where(fits, taper * jnp.where(row % SUB < HALF, cosine, sine), 0.0)


def sum_kernel(got_ref, phase_ref, out_ref, acc):
    tiles = got_ref.shape[0]
    acc[...] = jnp.zeros_like(acc)
    for sender in range(tiles):
        data = got_ref[sender, :SUB, :].astype(F32)
        ids = got_ref[sender, SUB:, :].astype(F32)[:1]
        for sub in range(SPP):
            at = slice(sub // 2 * SUB, (sub // 2 + 1) * SUB)
            lanes = slice(sub % 2 * 4 * SUB, (sub % 2 + 1) * 4 * SUB)
            acc[at, lanes] += jnp.where(ids == sub, data, 0.0)
    made = lax.dot_general(
        acc[...], fold_matrix(), (((1,), (0,)), ((), ())),
        precision=lax.Precision.HIGHEST, preferred_element_type=F32,
    )
    turned = pltpu.roll(made, 2 * SUB, 1)
    for pair in range(SPP // 2):
        at = slice(pair * SUB, (pair + 1) * SUB)
        other = SPP // 2 + pair
        out_ref[at, :] = (made[at] * phase_ref[pair : pair + 1] + turned[at] * phase_ref[other : other + 1]).astype(BF16)


def sum_subgrids(got, phase):
    vmem = pl.BlockSpec(memory_space=pltpu.VMEM)
    return pl.pallas_call(
        sum_kernel,
        in_specs=[vmem] * 2,
        out_specs=vmem,
        out_shape=jax.ShapeDtypeStruct((SPP // 2 * SUB, 4 * SUB), BF16),
        scratch_shapes=[pltpu.VMEM((SPP // 2 * SUB, 8 * SUB), F32)],
        compiler_params=pltpu.CompilerParams(vmem_limit_bytes=SMALL),
        name="sums",
    )(got, phase)


def column_phases(norm, tiles, ctrl_ref, w_ref, phase_ref):
    subs = SPP * tiles
    lane = lax.broadcasted_iota(jnp.int32, (SPP, 4 * SUB), 1)
    row = lax.broadcasted_iota(jnp.int32, (SPP, 4 * SUB), 0)
    column = lane % SUB
    odd = lane // SUB % 2
    first = jnp.zeros((SPP, 4 * SUB), jnp.int32)
    w = jnp.zeros((SPP, 4 * SUB), F32)
    for sub in range(SPP):
        here = (row % (SPP // 2) == sub // 2) & (odd == sub % 2)
        s = sub * tiles + ctrl_ref[3 * subs]
        first = jnp.where(here, ctrl_ref[subs + s], first)
        w = jnp.where(here, w_ref[0, ctrl_ref[2 * subs + s]], w)
    x = (first + column).astype(F32) / NCOL - 0.5
    turns = w * (x * x) - ((31 * column) & 63).astype(F32) / 64
    c_re, c_im = cis(turns - jnp.round(turns))
    c_im = jnp.where(lane < 2 * SUB, -c_im, c_im)
    phase_ref[...] = jnp.where(row < SPP // 2, c_re, c_im) * norm


def phase_kernel(norm, tiles, ctrl_ref, w_ref, mat_ref, turn_ref, base_ref, phase_ref):
    subs, rows = turn_ref.shape[1:]
    column_phases(norm, tiles, ctrl_ref, w_ref, phase_ref)
    first = ctrl_ref[3 * subs] * rows
    for k in range(subs):
        s = k % SPP * tiles + k // SPP
        turn_ref[0, k : k + 1, :] = jnp.full((1, rows), ctrl_ref[s].astype(F32))
        turn_ref[1, k : k + 1, :] = jnp.full((1, rows), w_ref[0, ctrl_ref[2 * subs + s]])
    gy = turn_ref[0].astype(jnp.int32)
    q = first + lax.broadcasted_iota(jnp.int32, (subs, rows), 1)
    steps = (q * gy + NV // 2) & (NV - 1)
    pos = q.astype(F32) / NV - 0.5
    turns = (NV // 2 - steps).astype(F32) / NV + turn_ref[1] * (pos * pos)
    turn_ref[0], turn_ref[1] = cis(turns - jnp.round(turns))
    q = first + lax.broadcasted_iota(jnp.int32, (SUB, rows), 1)
    r = lax.broadcasted_iota(jnp.int32, (SUB, rows), 0)
    steps = ((q + 31 * NV // 64) * r + NV // 2) & (NV - 1)
    for part, value in enumerate(cis((NV // 2 - steps).astype(F32) / NV)):
        base_ref[part] = lax.dot_general(
            mat_ref[...], value, (((1,), (0,)), ((), ())),
            precision=lax.Precision.HIGHEST, preferred_element_type=F32,
        )


def make_phases(ctrl, w_band, norm, tiles):
    rows = NV // tiles
    subs = SPP * tiles
    smem = pl.BlockSpec(memory_space=pltpu.SMEM)
    vmem = pl.BlockSpec(memory_space=pltpu.VMEM)
    return pl.pallas_call(
        functools.partial(phase_kernel, norm, tiles),
        in_specs=[smem] * 2 + [vmem],
        out_specs=[vmem] * 3,
        out_shape=[
            jax.ShapeDtypeStruct((2, subs, rows), F32),
            jax.ShapeDtypeStruct((2, SUB, rows), F32),
            jax.ShapeDtypeStruct((SPP, 4 * SUB), F32),
        ],
        compiler_params=pltpu.CompilerParams(vmem_limit_bytes=LIMIT),
        name="phases",
    )(ctrl, w_band, jnp.asarray(column_matrix().T, F32))


def image_kernel(tiles, sides, first_part, last_part, ctrl_ref, turn_ref, base_ref, *refs):
    zs, refs = refs[: len(sides)], refs[len(sides) :]
    start = None
    if not first_part:
        start, refs = refs[0], refs[1:]
    out_ref, refs = refs[0], refs[1:]
    acc = out_ref
    if last_part:
        acc, refs = refs[0], refs[1:]
    canvas, table = refs
    rows = turn_ref.shape[2]
    subs = SPP * tiles
    me = ctrl_ref[3 * subs]
    depth = tiles // 4
    lane = lax.broadcasted_iota(jnp.int32, (SUB, 4 * SUB), 1)
    base_re, base_im = base_ref[0], base_ref[1]
    acc[...] = jnp.zeros(acc.shape, F32) if first_part else start[...]
    for side, z_ref in zip(sides, zs):

        @pl.loop(0, depth, unroll=4)
        def _(t):
            panel = ((me // 4 - t) & (depth - 1)) * 4 + ((me & 3) ^ side)
            for pair in range(SPP // 2):
                z = z_ref[t, pair * SUB : (pair + 1) * SUB, :].astype(F32)
                for odd in range(2):
                    sub = 2 * pair + odd
                    first = ctrl_ref[subs + sub * tiles + panel]
                    moved = pltpu.roll(z, (first - odd * SUB + 4 * SUB) & (4 * SUB - 1), 1)
                    place = (lane & (NCOL - 1)) - first
                    canvas[sub * SUB : (sub + 1) * SUB, :] = jnp.where((place >= 0) & (place < SUB), moved, 0.0)
            turn_re = turn_ref[0, pl.ds(panel * SPP, SPP), :]
            turn_im = turn_ref[1, pl.ds(panel * SPP, SPP), :]
            for sub in range(SPP):
                at = slice(sub * SUB, (sub + 1) * SUB)
                t_re, t_im = turn_re[sub : sub + 1], turn_im[sub : sub + 1]
                table[at, :rows] = (t_re * base_re - t_im * base_im).astype(BF16)
                table[at, rows:] = (t_re * base_im + t_im * base_re).astype(BF16)
            acc[...] += jnp.dot(canvas[...].T.astype(BF16), table[...], preferred_element_type=F32)

    if last_part:
        real = acc[:NCOL, :rows] - acc[NCOL:, rows:]
        imag = acc[NCOL:, :rows] + acc[:NCOL, rows:]
        out_ref[...] = jnp.concatenate([real, imag], axis=0).T


def make_image(ctrl, turn, base, zs, sides, tiles, start=None, last=False):
    rows = turn.shape[2]
    smem = pl.BlockSpec(memory_space=pltpu.SMEM)
    vmem = pl.BlockSpec(memory_space=pltpu.VMEM)
    carry = [] if start is None else [start]
    scratch = [
        pltpu.VMEM((4 * SUB, 2 * rows), F32),
        pltpu.VMEM((SPP * SUB, 4 * SUB), F32),
        pltpu.VMEM((SPP * SUB, 2 * rows), BF16),
    ]
    return pl.pallas_call(
        functools.partial(image_kernel, tiles, sides, start is None, last),
        in_specs=[smem] + [vmem] * (2 + len(zs) + len(carry)),
        out_specs=vmem,
        out_shape=jax.ShapeDtypeStruct((rows, 4 * SUB) if last else (4 * SUB, 2 * rows), F32),
        scratch_shapes=scratch if last else scratch[1:],
        compiler_params=pltpu.CompilerParams(vmem_limit_bytes=SMALL),
        name="image",
    )(ctrl, turn, base, *zs, *carry)


def shards(vis, coords, block_fill, block_sub, sub_pos, sub_plane, freq, plane_w):
    tiles = lax.axis_size("tile")
    me = lax.axis_index("tile").reshape(1)
    norm = 1.0 / (math.sqrt(vis.shape[2] // 2 * vis.shape[3]) * SUB * math.sqrt(NV))
    skies = form_skies(vis[0], coords, block_fill, block_sub, freq, tiles)
    ctrl = jnp.concatenate([sub_pos[:, 0], sub_pos[:, 1], sub_plane, me])
    turn, base, phase = make_phases(ctrl, plane_w, norm, tiles)
    got = lax.all_to_all(skies, "tile", split_axis=0, concat_axis=0, tiled=True)
    z = sum_subgrids(got, phase)
    depth = tiles // 4
    ahead = lambda i, t: (i // 4 + t) % depth * 4 + i % 4
    moved = [lax.ppermute(z, "tile", [(i, ahead(i, t)) for i in range(tiles)]) for t in range(1, depth)]
    opposite = [(i, i ^ 2) for i in range(tiles)]
    beside = [(i, i ^ 1) for i in range(tiles)]
    facing = lax.ppermute(z, "tile", opposite)
    moved = jnp.stack(moved)
    others = lax.ppermute(moved, "tile", opposite)
    column = jnp.concatenate([z[None], moved])
    twin = lax.ppermute(column, "tile", beside)
    part = make_image(ctrl, turn, base, [column, twin], [0, 1], tiles)
    others, part = lax.optimization_barrier((others, part))
    across = jnp.concatenate([facing[None], others])
    far = lax.ppermute(across, "tile", beside)
    part = make_image(ctrl, turn, base, [across], [2], tiles, part)
    return make_image(ctrl, turn, base, [far], [3], tiles, part, True)[None]


def solution(mesh):
    return jax.shard_map(
        shards,
        mesh=mesh,
        in_specs=(
            P("band", "tile", None, None),
            P("tile", None, None),
            P("tile"),
            P("tile"),
            P(),
            P(),
            P("band", None),
            P("band", None),
        ),
        out_specs=P("band", "tile", None),
        check_vma=False,
    )
```
